128 devices in a mesh: fsdp: 32 (over y, z_hi, x), tensor: 4 (over z_lo, core).
Axes of the slice: x: 4, y: 4, z: 4 (z_hi: 2, z_lo: 2; z = z_hi * 2 + z_lo), core: 2. Of those that a mesh axis runs over, the one named last changes fastest.
Arguments:
- images: bfloat16 [256, 14, 14, 512], P('fsdp'), may hold values from -6 to 6
- out_grad: bfloat16 [256, 14, 14, 512], P('fsdp'), may hold values from -6 to 6
- rel_index: int32 [49, 49], replicated, may hold values from 0 to 168
- attn_weight: float32 [512, 3, 512], P('fsdp', None, 'tensor'), may hold values from -0.25 to 0.25
- attn_first: float32 [512, 3, 512], P('fsdp', None, 'tensor'), may hold values from -112 to 112
- attn_second: float32 [512, 3, 512], P('fsdp', None, 'tensor'), may hold values from 25.088 to 100.352
- proj_weight: float32 [512, 512], P('tensor', 'fsdp'), may hold values from -1 to 1
- proj_first: float32 [512, 512], P('tensor', 'fsdp'), may hold values from -32 to 32
- proj_second: float32 [512, 512], P('tensor', 'fsdp'), may hold values from 3.01056 to 12.04224
- up_weight: float32 [512, 2048], P('fsdp', 'tensor'), may hold values from -0.25 to 0.25
- up_first: float32 [512, 2048], P('fsdp', 'tensor'), may hold values from -48 to 48
- up_second: float32 [512, 2048], P('fsdp', 'tensor'), may hold values from 4.51584 to 18.06336
- down_weight: float32 [2048, 512], P('tensor', 'fsdp'), may hold values from -0.125 to 0.125
- down_first: float32 [2048, 512], P('tensor', 'fsdp'), may hold values from -96 to 96
- down_second: float32 [2048, 512], P('tensor', 'fsdp'), may hold values from 18.06336 to 72.25344
- vectors: float32 [6, 512], replicated, may hold values from -4 to 4
- vec_first: float32 [6, 512], replicated, may hold values from -160 to 160
- vec_second: float32 [6, 512], replicated, may hold values from 50.176 to 200.704
- head_bias: float32 [2, 512], P(None, 'tensor'), may hold values from -4 to 4
- head_first: float32 [2, 512], P(None, 'tensor'), may hold values from -112 to 112
- head_second: float32 [2, 512], P(None, 'tensor'), may hold values from 25.088 to 100.352
- unit_bias: float32 [2048], P('tensor'), may hold values from -4 to 4
- unit_first: float32 [2048], P('tensor'), may hold values from -48 to 48
- unit_second: float32 [2048], P('tensor'), may hold values from 4.51584 to 18.06336
- rel_table: float32 [169, 16], P(None, 'tensor'), may hold values from -6 to 6
- table_first: float32 [169, 16], P(None, 'tensor'), may hold values from -40 to 40
- table_second: float32 [169, 16], P(None, 'tensor'), may hold values from 3.51232 to 14.04928
Outputs:
- block_out: bfloat16 [256, 14, 14, 512], P('fsdp')
- images_grad: float32 [256, 14, 14, 512], P('fsdp')
- attn_new: float32 [512, 3, 512], P('fsdp', None, 'tensor')
- attn_moment: float32 [512, 3, 512], P('fsdp', None, 'tensor')
- attn_square: float32 [512, 3, 512], P('fsdp', None, 'tensor')
- proj_new: float32 [512, 512], P('tensor', 'fsdp')
- proj_moment: float32 [512, 512], P('tensor', 'fsdp')
- proj_square: float32 [512, 512], P('tensor', 'fsdp')
- up_new: float32 [512, 2048], P('fsdp', 'tensor')
- up_moment: float32 [512, 2048], P('fsdp', 'tensor')
- up_square: float32 [512, 2048], P('fsdp', 'tensor')
- down_new: float32 [2048, 512], P('tensor', 'fsdp')
- down_moment: float32 [2048, 512], P('tensor', 'fsdp')
- down_square: float32 [2048, 512], P('tensor', 'fsdp')
- vec_new: float32 [6, 512], replicated
- vec_moment: float32 [6, 512], replicated
- vec_square: float32 [6, 512], replicated
- head_new: float32 [2, 512], P(None, 'tensor')
- head_moment: float32 [2, 512], P(None, 'tensor')
- head_square: float32 [2, 512], P(None, 'tensor')
- unit_new: float32 [2048], P('tensor')
- unit_moment: float32 [2048], P('tensor')
- unit_square: float32 [2048], P('tensor')
- table_new: float32 [169, 16], P(None, 'tensor')
- table_moment: float32 [169, 16], P(None, 'tensor')
- table_square: float32 [169, 16], P(None, 'tensor')
The draws below stay inside these ranges and needn't reach their ends.
Inputs may be any that keep to these rules, and one draw needn't show every extreme that they name: `rel_index`: each entry names a row of rel_table.
All inputs are finite; a program needn't handle non-finite values.
Results may differ from the reference program's by a relative error of at most 0.012.
Values may be sent and summed in bfloat16 or wider, within the bound.
A program may use at most 128 MiB of HBM per device.

```python
import math
import jax
import jax.numpy as jnp
from jax import lax

D = 512
HEADS = 16
HD = 32
FF = 2048
IMG_DEV = 8
SIDE = 14
WIN = 7
STEP = 10
IMAGES = 256
TOKENS = 50176
REL = 169


def with_ends(values, key, least, largest):
    longest = values.shape.index(max(values.shape))
    spots = []
    for shift in (0, 1):
        where = [jax.random.randint(jax.random.fold_in(key, axis), (), 0, length) for axis, length in enumerate(values.shape)]
        where[longest] = (where[longest] + shift) % values.shape[longest]
        spots.append(tuple(where))
    return values.at[spots[0]].set(least).at[spots[1]].set(largest)


def steps_of(rng, dims, shards, least, largest):
    gain, own = 1.0, jax.random.fold_in(rng, 6)
    for axis_at, shards_of in shards:
        heights = jnp.exp(jax.random.uniform(jax.random.fold_in(own, axis_at), (shards_of,), jnp.float32, least / len(shards), largest / len(shards)))
        gain = gain * jnp.repeat(heights, dims[axis_at] // shards_of).reshape([-1 if axis == axis_at else 1 for axis in range(len(dims))])
    return gain


def normal_values(stream_key, dims, width, bound, pieces=(), held_as=jnp.bfloat16):
    values = width * jax.random.normal(stream_key, dims, jnp.float32)
    if pieces:
        values = values * steps_of(stream_key, dims, pieces, -0.22, 0.18)
    return jnp.clip(values, -bound, bound).astype(held_as)


def setup_inputs(seed: int = 0) -> dict:
    key_of = jax.random.split(jax.random.key(seed), 28)
    images = normal_values(key_of[0], (IMAGES, SIDE, SIDE, D), 1.0, 6.0, ((0, 32),))
    out_grad = normal_values(key_of[1], (IMAGES, SIDE, SIDE, D), 1.0, 6.0, ((0, 32),))
    rel_index = with_ends(jax.random.randint(key_of[2], (WIN * WIN, WIN * WIN), 0, REL), jax.random.fold_in(key_of[2], 1), 0, REL - 1).astype(jnp.int32)
    attn_weight = normal_values(key_of[3], (D, 3, D), D ** -0.5, 0.25, ((0, 32), (2, 4)), jnp.float32)
    attn_first = normal_values(key_of[4], (D, 3, D), (0.11 * (0.5 * TOKENS) ** 0.5), 112.0, ((0, 32), (2, 4)), jnp.float32)
    attn_second = jnp.clip(jnp.exp(math.log(100.352) - 1.3862944 * jax.random.uniform(key_of[5], (D, 3, D), jnp.float32) ** steps_of(key_of[5], (D, 3, D), ((0, 32), (2, 4)), -0.2, 0.2)), 25.088, 100.352)
    proj_weight = normal_values(key_of[6], (D, D), (D // 16) ** -0.5, 1.0, ((0, 4), (1, 32)), jnp.float32)
    proj_first = normal_values(key_of[7], (D, D), (0.11 * (0.06 * TOKENS) ** 0.5), 32.0, ((0, 4), (1, 32)), jnp.float32)
    proj_second = jnp.clip(jnp.exp(math.log(12.04224) - 1.3862944 * jax.random.uniform(key_of[8], (D, D), jnp.float32) ** steps_of(key_of[8], (D, D), ((0, 4), (1, 32)), -0.2, 0.2)), 3.01056, 12.04224)
    up_weight = normal_values(key_of[9], (D, FF), D ** -0.5, 0.25, ((0, 32), (1, 4)), jnp.float32)
    up_first = normal_values(key_of[10], (D, FF), (0.11 * (0.09 * TOKENS) ** 0.5), 48.0, ((0, 32), (1, 4)), jnp.float32)
    up_second = jnp.clip(jnp.exp(math.log(18.06336) - 1.3862944 * jax.random.uniform(key_of[11], (D, FF), jnp.float32) ** steps_of(key_of[11], (D, FF), ((0, 32), (1, 4)), -0.2, 0.2)), 4.51584, 18.06336)
    down_weight = normal_values(key_of[12], (FF, D), FF ** -0.5, 0.125, ((0, 4), (1, 32)), jnp.float32)
    down_first = normal_values(key_of[13], (FF, D), (0.11 * (0.36 * TOKENS) ** 0.5), 96.0, ((0, 4), (1, 32)), jnp.float32)
    down_second = jnp.clip(jnp.exp(math.log(72.25344) - 1.3862944 * jax.random.uniform(key_of[14], (FF, D), jnp.float32) ** steps_of(key_of[14], (FF, D), ((0, 4), (1, 32)), -0.2, 0.2)), 18.06336, 72.25344)
    vectors = normal_values(key_of[15], (6, D), 0.3, 4.0, (), jnp.float32)
    vec_first = normal_values(key_of[16], (6, D), (0.11 * (1.0 * TOKENS) ** 0.5), 160.0, (), jnp.float32)
    vec_second = jnp.clip(jnp.exp(jax.random.uniform(key_of[17], (6, D), jnp.float32, math.log(50.176), math.log(200.704))), 50.176, 200.704)
    head_bias = normal_values(key_of[18], (2, D), 0.3, 4.0, ((1, 4),), jnp.float32)
    head_first = normal_values(key_of[19], (2, D), (0.11 * (0.5 * TOKENS) ** 0.5), 112.0, ((1, 4),), jnp.float32)
    head_second = jnp.clip(jnp.exp(math.log(100.352) - 1.3862944 * jax.random.uniform(key_of[20], (2, D), jnp.float32) ** steps_of(key_of[20], (2, D), ((1, 4),), -0.2, 0.2)), 25.088, 100.352)
    unit_bias = normal_values(key_of[21], (FF,), 0.3, 4.0, ((0, 4),), jnp.float32)
    unit_first = normal_values(key_of[22], (FF,), (0.11 * (0.09 * TOKENS) ** 0.5), 48.0, ((0, 4),), jnp.float32)
    unit_second = jnp.clip(jnp.exp(math.log(18.06336) - 1.3862944 * jax.random.uniform(key_of[23], (FF,), jnp.float32) ** steps_of(key_of[23], (FF,), ((0, 4),), -0.2, 0.2)), 4.51584, 18.06336)
    rel_table = normal_values(key_of[24], (REL, HEADS), 1.0, 6.0, ((1, 4),), jnp.float32)
    table_first = normal_values(key_of[25], (REL, HEADS), (0.11 * (0.07 * TOKENS) ** 0.5), 40.0, ((1, 4),), jnp.float32)
    table_second = jnp.clip(jnp.exp(math.log(14.04928) - 1.3862944 * jax.random.uniform(key_of[26], (REL, HEADS), jnp.float32) ** steps_of(key_of[26], (REL, HEADS), ((1, 4),), -0.2, 0.2)), 3.51232, 14.04928)
    return {"images": images, "out_grad": out_grad, "rel_index": rel_index, "attn_weight": attn_weight, "attn_first": attn_first, "attn_second": attn_second, "proj_weight": proj_weight, "proj_first": proj_first, "proj_second": proj_second, "up_weight": up_weight, "up_first": up_first, "up_second": up_second, "down_weight": down_weight, "down_first": down_first, "down_second": down_second, "vectors": vectors, "vec_first": vec_first, "vec_second": vec_second, "head_bias": head_bias, "head_first": head_first, "head_second": head_second, "unit_bias": unit_bias, "unit_first": unit_first, "unit_second": unit_second, "rel_table": rel_table, "table_first": table_first, "table_second": table_second}


@jax.custom_vjp
def low(v):
    return lax.optimization_barrier(v.astype(jnp.bfloat16)).astype(jnp.float32)

@jax.custom_vjp
def low_back(v):
    return v

def low_keep(v):
    return (low(v), None)

def low_pass(kept, grad):
    return (grad,)

def back_keep(v):
    return (v, None)

def back_low(kept, grad):
    return (low(grad),)
low.defvjp(low_keep, low_pass)
low_back.defvjp(back_keep, back_low)
NORM_EPS = 1e-05
BETA_ONE = 0.9
BETA_TWO = 0.999
ADAM_EPS = 1e-08
RATE_MATRIX = 0.1
RATE_VECTOR = 0.2
RATE_TABLE = 0.5
WEIGHT_DECAY = 0.05

def layer_norm(values, offset, shift):
    center = values - lax.optimization_barrier(jnp.mean(values, axis=-1, keepdims=True))
    spread = lax.optimization_barrier(jnp.mean(center * center, axis=-1, keepdims=True))
    return center * lax.rsqrt(spread + NORM_EPS) * (1.0 + offset) + shift

def to_windows(field):
    count = field.shape[0]
    split = field.reshape(count, SIDE // WIN, WIN, SIDE // WIN, WIN, field.shape[-1])
    return split.transpose(0, 1, 3, 2, 4, 5).reshape(-1, WIN * WIN, field.shape[-1])

def from_windows(field, count):
    split = field.reshape(count, SIDE // WIN, SIDE // WIN, WIN, WIN, field.shape[-1])
    return split.transpose(0, 1, 3, 2, 4, 5).reshape(count, SIDE, SIDE, field.shape[-1])

def forward(field, weights, rel_index):
    attn_weight, proj_weight, up_weight, down_weight, vectors, head_bias, unit_bias, rel_table = weights
    highest = lax.Precision.HIGHEST
    tokens = to_windows(field)
    windows = tokens.shape[0]
    heads_shape = (windows, WIN * WIN, HEADS, HD)
    norm_one = low(layer_norm(tokens, vectors[0], vectors[1]))
    mixed = jnp.einsum('wtd,dce->wtce', norm_one, low(attn_weight), precision=highest)
    query = low_back(low(mixed[:, :, 0] + head_bias[0])).reshape(heads_shape)
    keys = low_back(low(mixed[:, :, 1])).reshape(heads_shape)
    values = low_back(low(mixed[:, :, 2] + head_bias[1])).reshape(heads_shape)
    pos_bias = jnp.transpose(rel_table[rel_index], (2, 0, 1))
    raw = jnp.einsum('wqhe,wkhe->whqk', query, keys, precision=highest)
    scores = low_back(raw * float(HD) ** (-0.5) + pos_bias)
    probs = low(jax.nn.softmax(scores, axis=-1))
    attended = jnp.einsum('whqk,wkhe->wqhe', probs, values, precision=highest)
    attended = low_back(low(attended.reshape(windows, WIN * WIN, D)))
    branch = low_back(jnp.einsum('wte,ed->wtd', attended, low(proj_weight), precision=highest))
    middle = tokens + (branch + vectors[2])
    norm_two = low(layer_norm(middle, vectors[3], vectors[4]))
    pre = low_back(jnp.einsum('wtd,df->wtf', norm_two, low(up_weight), precision=highest)) + unit_bias
    hidden = low(jax.nn.gelu(pre, approximate=False))
    result = middle + (jnp.einsum('wtf,fd->wtd', hidden, low(down_weight), precision=highest) + vectors[5])
    return from_windows(result, field.shape[0])

def adam_step(weight, grad, first, second, rate, decay):
    first_new = BETA_ONE * first + (1.0 - BETA_ONE) * grad
    second_new = BETA_TWO * second + (1.0 - BETA_TWO) * grad * grad
    first_hat = first_new / (1.0 - BETA_ONE ** STEP)
    second_hat = second_new / (1.0 - BETA_TWO ** STEP)
    updated = weight - rate * (first_hat / (jnp.sqrt(second_hat) + ADAM_EPS) + decay * weight)
    return (updated, first_new, second_new)

def reference(images, out_grad, rel_index, attn_weight, attn_first, attn_second, proj_weight, proj_first, proj_second, up_weight, up_first, up_second, down_weight, down_first, down_second, vectors, vec_first, vec_second, head_bias, head_first, head_second, unit_bias, unit_first, unit_second, rel_table, table_first, table_second):
    params = (attn_weight, proj_weight, up_weight, down_weight, vectors, head_bias, unit_bias, rel_table)
    groups = images.shape[0] // IMG_DEV
    fields = images.astype(jnp.float32).reshape(groups, IMG_DEV, SIDE, SIDE, D)
    cotangents = out_grad.astype(jnp.float32).reshape(groups, IMG_DEV, SIDE, SIDE, D)

    def run(field, weights):
        return forward(field, weights, rel_index)

    def one_group(totals, pair):
        result, pull = jax.vjp(run, pair[0], params)
        field_grad, weight_grads = pull(pair[1])
        summed = tuple((a + b for a, b in zip(totals, weight_grads)))
        return (summed, (result.astype(jnp.bfloat16), field_grad))
    start = tuple((jnp.zeros_like(p) for p in params))
    totals, (results, field_grads) = lax.scan(one_group, start, (fields, cotangents))
    block_out = results.reshape(images.shape)
    images_grad = field_grads.reshape(images.shape)
    attn_new, attn_moment, attn_square = adam_step(attn_weight, totals[0], attn_first, attn_second, RATE_MATRIX, WEIGHT_DECAY)
    proj_new, proj_moment, proj_square = adam_step(proj_weight, totals[1], proj_first, proj_second, RATE_MATRIX, WEIGHT_DECAY)
    up_new, up_moment, up_square = adam_step(up_weight, totals[2], up_first, up_second, RATE_MATRIX, WEIGHT_DECAY)
    down_new, down_moment, down_square = adam_step(down_weight, totals[3], down_first, down_second, RATE_MATRIX, WEIGHT_DECAY)
    vec_new, vec_moment, vec_square = adam_step(vectors, totals[4], vec_first, vec_second, RATE_VECTOR, 0.0)
    head_new, head_moment, head_square = adam_step(head_bias, totals[5], head_first, head_second, RATE_VECTOR, 0.0)
    unit_new, unit_moment, unit_square = adam_step(unit_bias, totals[6], unit_first, unit_second, RATE_VECTOR, 0.0)
    table_new, table_moment, table_square = adam_step(rel_table, totals[7], table_first, table_second, RATE_TABLE, 0.0)
    return (block_out, images_grad, attn_new, attn_moment, attn_square, proj_new, proj_moment, proj_square, up_new, up_moment, up_square, down_new, down_moment, down_square, vec_new, vec_moment, vec_square, head_new, head_moment, head_square, unit_new, unit_moment, unit_square, table_new, table_moment, table_square)
```

```python
import functools

import jax
import jax.numpy as jnp
from jax import lax
from jax.experimental import pallas as pl
from jax.experimental.pallas import tpu as pltpu
from jax.sharding import PartitionSpec as P

MESH = pl.DeviceIdType.MESH
ORDERS = ((0, 1, 2), (1, 2, 0), (2, 0, 1))


class Place:
    def __init__(self):
        f = lax.axis_index("fsdp")
        t = lax.axis_index("tensor")
        self.x = f % 4
        self.y = f // 8
        self.z = ((f // 4) % 2) * 2 + t // 2
        self.core = t % 2
        self.at = (self.x, self.y, self.z)
        self.step = 1 - 2 * self.core

    def device(self, at=None, core=None):
        x, y, z = self.at if at is None else at
        core = self.core if core is None else core
        return (y * 8 + (z // 2) * 4 + x, (z % 2) * 2 + core)

    def along(self, axis, by):
        at = list(self.at)
        at[axis] = (at[axis] + by + 4) % 4
        return self.device(at)

    def sibling(self):
        return self.device(core=1 - self.core)

    def partners(self):
        ring = [self.along(axis, by) for axis in range(3) for by in (1, 3)]
        other_z = (self.z // 2) * 2 + 1 - self.z % 2
        across = self.device((self.x, self.y, other_z), 1 - self.core)
        return ring + [self.sibling(), across]


def greet(place):
    barrier = pltpu.get_barrier_semaphore()
    partners = place.partners()
    for device in partners:
        pl.semaphore_signal(barrier, inc=1, device_id=device, device_id_type=MESH)
    pl.semaphore_wait(barrier, len(partners))


def block_of(ref, lead, place, core, done, axis=None, shift=0):
    full = slice(None)
    at = list(place.at)
    if axis is not None:
        at[axis] = (at[axis] + shift + 4) % 4
    x, y, z = at
    x = full if 0 in done else x
    y = full if 1 in done else y
    zl, zh = (full, full) if 2 in done else (z % 2, z // 2)
    index = (*lead, zl, core, y, zh, x) if core is not None else (*lead, zl, y, zh, x)
    return ref.at[index]


def gather_kernel(w_ref, s_ref, gw_ref, gs_ref, own_sem, out_sem, in_sem, sib_out, sib_in, small_out, small_in):
    place = Place()
    core, step = place.core, place.step
    t = lax.axis_index("tensor")
    greet(place)
    other_z = (place.z // 2) * 2 + 1 - place.z % 2
    mates = [
        place.sibling(),
        place.device((place.x, place.y, other_z)),
        place.device((place.x, place.y, other_z), 1 - core),
    ]
    small = []
    for k, mate in enumerate(mates):
        copy = pltpu.make_async_remote_copy(s_ref, gs_ref.at[t], small_out.at[k], small_in.at[k], mate, MESH)
        copy.start()
        small.append(copy)
    small_own = pltpu.make_async_copy(s_ref, gs_ref.at[t], own_sem.at[3])
    small_own.start()

    def send(src, dst, slot, outs, ins, device):
        copy = pltpu.make_async_remote_copy(src, dst, outs.at[slot], ins.at[slot], device, MESH)
        copy.start()
        return copy

    waits = []
    own = []
    for p in range(3):
        mine = block_of(gw_ref, (p,), place, core, ())
        copy = pltpu.make_async_copy(w_ref.at[p], mine, own_sem.at[p])
        copy.start()
        own.append(copy)
    for p in range(3):
        own[p].wait()
        mine = block_of(gw_ref, (p,), place, core, ())
        waits.append(send(mine, mine, (p, 3, 0), sib_out, sib_in, place.sibling()))
    for phase in range(3):
        for p in range(3):
            axis, done = ORDERS[p][phase], ORDERS[p][:phase]
            mine = block_of(gw_ref, (p,), place, core, done)
            waits.append(send(mine, mine, (p, phase, 0), out_sem, in_sem, place.along(axis, step)))
            waits.append(send(mine, mine, (p, phase, 1), out_sem, in_sem, place.along(axis, -step)))
        def arrived(p, phase, kind, shift):
            axis, done = ORDERS[p][phase], ORDERS[p][:phase]
            block = block_of(gw_ref, (p,), place, core, done, axis, shift)
            pltpu.make_async_remote_copy(
                block, block, out_sem.at[p, phase, kind], in_sem.at[p, phase, kind], place.sibling(), MESH
            ).wait_recv()
            return block
        for p in range(3):
            axis = ORDERS[p][phase]
            block = arrived(p, phase, 0, -step)
            waits.append(send(block, block, (p, phase, 2), out_sem, in_sem, place.along(axis, step)))
            waits.append(send(block, block, (p, phase, 0), sib_out, sib_in, place.sibling()))
        for p in range(3):
            block = arrived(p, phase, 1, step)
            waits.append(send(block, block, (p, phase, 1), sib_out, sib_in, place.sibling()))
        for p in range(3):
            block = arrived(p, phase, 2, 2)
            waits.append(send(block, block, (p, phase, 2), sib_out, sib_in, place.sibling()))
    for p in range(3):
        block = block_of(gw_ref, (p,), place, 1 - core, ())
        pltpu.make_async_remote_copy(block, block, sib_out.at[p, 3, 0], sib_in.at[p, 3, 0], place.sibling(), MESH).wait_recv()
        for phase in range(3):
            axis, done = ORDERS[p][phase], ORDERS[p][:phase]
            for kind, shift in enumerate((step, -step, 2)):
                block = block_of(gw_ref, (p,), place, 1 - core, done, axis, shift)
                pltpu.make_async_remote_copy(
                    block, block, sib_out.at[p, phase, kind], sib_in.at[p, phase, kind], place.sibling(), MESH
                ).wait_recv()
    for copy in waits:
        copy.wait_send()
    small_own.wait()
    for copy in small:
        copy.wait()


def gather(w, s):
    return pl.pallas_call(
        gather_kernel,
        out_shape=(
            jax.ShapeDtypeStruct((3, 2, 2, 4, 2, 4, 16, 512), jnp.bfloat16),
            jax.ShapeDtypeStruct((4, 16, 128), jnp.float32),
        ),
        in_specs=[pl.BlockSpec(memory_space=pl.ANY)] * 2,
        out_specs=[pl.BlockSpec(memory_space=pl.ANY)] * 2,
        scratch_shapes=[
            pltpu.SemaphoreType.DMA((4,)),
            pltpu.SemaphoreType.DMA((3, 3, 3)),
            pltpu.SemaphoreType.DMA((3, 3, 3)),
            pltpu.SemaphoreType.DMA((3, 4, 3)),
            pltpu.SemaphoreType.DMA((3, 4, 3)),
            pltpu.SemaphoreType.DMA((3,)),
            pltpu.SemaphoreType.DMA((3,)),
        ],
        compiler_params=pltpu.CompilerParams(collective_id=0, has_side_effects=True),
        name="gather_weights",
    )(w, s)


LOW = jnp.bfloat16
FULL = jnp.float32
EPS = 1e-5
SCALE = 32.0 ** -0.5
BLOCKED = -1e30


def mm(a, b):
    return lax.dot_general(a, b, (((1,), (0,)), ((), ())), preferred_element_type=FULL)


def mm_nt(a, b):
    return lax.dot_general(a, b, (((1,), (1,)), ((), ())), preferred_element_type=FULL)


def mm_tn(a, b):
    return lax.dot_general(a, b, (((0,), (0,)), ((), ())), preferred_element_type=FULL)


def three_lows(a):
    high = a.astype(LOW)
    rest = a - high.astype(FULL)
    middle = rest.astype(LOW)
    last = (rest - middle.astype(FULL)).astype(LOW)
    return jnp.concatenate([high, middle, last], axis=0)


def normed(v):
    center = v - jnp.mean(v, axis=-1, keepdims=True)
    r = lax.rsqrt(jnp.mean(center * center, axis=-1, keepdims=True) + EPS)
    return center * r, r


def norm_back(n, x, r, offset):
    q = n * (1.0 + offset)
    return r * (q - jnp.mean(q, axis=-1, keepdims=True) - x * jnp.mean(q * x, axis=-1, keepdims=True))


def gelu_parts(u):
    size = jnp.abs(u)
    k = 1.0 / (1.0 + (0.3275911 * 0.7071067811865476) * size)
    bell = jnp.exp(-0.5 * u * u)
    poly = k * (0.254829592 + k * (-0.284496736 + k * (1.421413741 + k * (-1.453152027 + k * 1.061405429))))
    tail = 0.5 * poly * bell
    share = jnp.where(u < 0, tail, 1.0 - tail)
    return u * share, share + u * bell * 0.3989422804014327


def lane_mask(h):
    lane = lax.broadcasted_iota(jnp.int32, (128, 128), 1)
    return (lane >= h * 32) & (lane < h * 32 + 32)


def keep(mask, a):
    return jnp.where(mask, a, jnp.zeros_like(a))


def middle_kernel(
    images, cotangents, gw, gs, vec, idx,
    grads, block, igrad, small,
    img_in, cot_in, w, tok, cot, cot_low, cot_t, n1, n1_t, x1, r1, n2, n2_t, x2, r2,
    qkv, probs, att, mid, hid, gpre, gmid, gml, gml_t, dqkv, onehot, spread, bias, dsum, table, field, sems,
    mine,
):
    first = mine()
    in_copies = [
        pltpu.make_async_copy(images.at[pl.ds(first, 2)], img_in, sems.at[0]),
        pltpu.make_async_copy(cotangents.at[pl.ds(first, 2)], cot_in, sems.at[1]),
    ]
    w_copies = [pltpu.make_async_copy(gw.at[p], w.at[p], sems.at[2 + p]) for p in range(3)]
    for copy in in_copies + w_copies:
        copy.start()
    small[...] = jnp.zeros((16, 768), FULL)
    tok[...] = jnp.zeros((512, 512), FULL)
    cot[...] = jnp.zeros((512, 512), FULL)
    for t in range(4):
        table[t * 4 : t * 4 + 4, 0:128] = gs[t, 0:4, :]
        table[t * 4 : t * 4 + 4, 128:256] = gs[t, 4:8, :]
    row_id = lax.broadcasted_iota(jnp.int32, (256, 128), 0)
    for i in range(49):
        onehot[:, i * 128 : (i + 1) * 128] = (row_id == idx[i : i + 1, :]).astype(FULL).astype(LOW)
    parts = three_lows(table[...])
    spread[...] = mm(parts, onehot[...])
    lane = lax.broadcasted_iota(jnp.int32, (16, 128), 1)
    low_side = lane < 49
    high_side = (lane >= 64) & (lane < 113)
    for i in range(64):
        if i < 49:
            at = slice(i * 128, (i + 1) * 128)
            line = spread[0:16, at] + spread[16:32, at] + spread[32:48, at]
        else:
            line = jnp.zeros((16, 128), FULL)
        bias[i * 16 : (i + 1) * 16, :] = jnp.where(low_side, line, BLOCKED)
        bias[(64 + i) * 16 : (65 + i) * 16, :] = jnp.where(high_side, line, BLOCKED)
    for copy in in_copies:
        copy.wait()

    for i in range(28):
        image, r = i // 14, i % 14
        top = (image * 4 + (r // 7) * 2) * 64 + (r % 7) * 7
        for side, (src, dst) in enumerate(((img_in, tok), (cot_in, cot))):
            page = field.at[(2 * i + side) % 4]
            page[0:14, :] = src[image, r].astype(FULL)
            dst[top : top + 7, :] = page[0:7, :]
            dst[top + 64 : top + 71, :] = page[7:14, :]

    def start(k, _):
        rows = pl.ds(pl.multiple_of(k * 64, 64), 64)
        x, r = normed(tok[rows, :])
        x1[rows, :] = x
        r1[rows, :] = r
        n1[rows, :] = (x * (1.0 + vec[0:1, :]) + vec[1:2, :]).astype(LOW)
        c = cot[rows, :]
        cot_low[rows, :] = c.astype(LOW)
        small[5:6, 0:512] += jnp.sum(c, axis=0, keepdims=True)
        return 0

    lax.fori_loop(0, 8, start, 0)
    n1_t[...] = n1[...].T
    cot_t[...] = cot_low[...].T
    w_copies[0].wait()

    def forward(t, _):
        mixed = mm(n1[...], w[0, t, :, 0:384])
        q_bias, v_bias = gs[t, 8:9, :], gs[t, 9:10, :]
        qkv[t, 0] = (mixed[:, 0:128] + q_bias).astype(LOW)
        qkv[t, 1] = mixed[:, 128:256].astype(LOW)
        qkv[t, 2] = (mixed[:, 256:384] + v_bias).astype(LOW)
        for wp in range(4):
            rows = slice(wp * 128, (wp + 1) * 128)
            q, k, v = qkv[t, 0, rows], qkv[t, 1, rows], qkv[t, 2, rows]
            ps, vs = [], []
            for h in range(4):
                mask = lane_mask(h)
                s = mm_nt(keep(mask, q), k) * SCALE + bias[pl.ds(t * 4 + h, 128, stride=16), :]
                e = jnp.exp(s - jnp.max(s, axis=-1, keepdims=True))
                p = (e / jnp.sum(e, axis=-1, keepdims=True)).astype(LOW)
                probs[t, wp, h] = p
                ps.append(p)
                vs.append(keep(mask, v))
            att[t, rows] = mm(jnp.concatenate(ps, axis=1), jnp.concatenate(vs, axis=0)).astype(LOW)
        return 0

    lax.fori_loop(0, 4, forward, 0)

    def second(k, _):
        rows = pl.ds(pl.multiple_of(k * 128, 128), 128)
        acc = tok[rows, :] + vec[2:3, :]
        for t in range(4):
            acc = acc + mm_nt(att[t, rows, :], w[0, t, :, 384:512])
        mid[rows, :] = acc
        x, r = normed(acc)
        x2[rows, :] = x
        r2[rows, :] = r
        n2[rows, :] = (x * (1.0 + vec[3:4, :]) + vec[4:5, :]).astype(LOW)
        return 0

    lax.fori_loop(0, 4, second, 0)
    n2_t[...] = n2[...].T
    w_copies[1].wait()
    w_copies[2].wait()

    def feed(t, _):
        unit = jnp.concatenate([gs[t, 10 + k : 11 + k, :] for k in range(4)], axis=1)

        def rows_of(k, total):
            rows = pl.ds(pl.multiple_of(k * 128, 128), 128)
            pre = mm(n2[rows, :], w[1, t]) + unit
            value, slope = gelu_parts(pre)
            hid[t, rows, :] = value.astype(LOW)
            g = mm(cot_low[rows, :], w[2, t]) * slope
            gpre[t, rows, :] = g.astype(LOW)
            return total + jnp.sum(g, axis=0, keepdims=True)

        small[pl.ds(8 + t, 1), 0:512] = lax.fori_loop(0, 4, rows_of, jnp.zeros((1, 512), FULL))
        grads[1, t] = mm(n2_t[...], gpre[t]).astype(LOW)
        grads[2, t] = mm(cot_t[...], hid[t]).astype(LOW)
        return 0

    lax.fori_loop(0, 4, feed, 0)

    def third(k, _):
        rows = pl.ds(pl.multiple_of(k * 128, 128), 128)
        out = mid[rows, :] + vec[5:6, :]
        n = jnp.zeros((128, 512), FULL)
        for t in range(4):
            out = out + mm_nt(hid[t, rows, :], w[2, t])
            n = n + mm_nt(gpre[t, rows, :], w[1, t])
        mid[rows, :] = out
        x = x2[rows, :]
        g = cot[rows, :] + norm_back(n, x, r2[rows, :], vec[3:4, :])
        gmid[rows, :] = g
        gml[rows, :] = g.astype(LOW)
        small[2:3, 0:512] += jnp.sum(g, axis=0, keepdims=True)
        small[3:4, 0:512] += jnp.sum(n * x, axis=0, keepdims=True)
        small[4:5, 0:512] += jnp.sum(n, axis=0, keepdims=True)
        return 0

    lax.fori_loop(0, 4, third, 0)
    gml_t[...] = gml[...].T

    def backward(t, _):
        ga = mm(gml[...], w[0, t, :, 384:512]).astype(LOW)
        grads[0, t, :, 384:512] = mm(gml_t[...], att[t]).astype(LOW)
        sums = [jnp.zeros((128, 128), FULL) for _ in range(4)]
        sum_q = jnp.zeros((1, 128), FULL)
        sum_v = jnp.zeros((1, 128), FULL)
        for wp in range(4):
            rows = slice(wp * 128, (wp + 1) * 128)
            q, k, v, g = qkv[t, 0, rows], qkv[t, 1, rows], qkv[t, 2, rows], ga[rows]
            dss, ps, ks, qs, gg = [], [], [], [], []
            for h in range(4):
                mask = lane_mask(h)
                p_low = probs[t, wp, h]
                p = p_low.astype(FULL)
                gh = keep(mask, g)
                dp = mm_nt(gh, v)
                ds = (p * (dp - jnp.sum(dp * p, axis=-1, keepdims=True))).astype(LOW)
                sums[h] = sums[h] + ds.astype(FULL)
                dss.append(ds)
                ps.append(p_low)
                ks.append(keep(mask, k))
                qs.append(keep(mask, q))
                gg.append(gh)
            dq = (mm(jnp.concatenate(dss, axis=1), jnp.concatenate(ks, axis=0)) * SCALE).astype(LOW)
            dk = (mm_tn(jnp.concatenate(dss, axis=0), jnp.concatenate(qs, axis=0)) * SCALE).astype(LOW)
            dv = mm_tn(jnp.concatenate(ps, axis=0), jnp.concatenate(gg, axis=0)).astype(LOW)
            dqkv[t, rows, 0:128] = dq
            dqkv[t, rows, 128:256] = dk
            dqkv[t, rows, 256:384] = dv
            sum_q = sum_q + jnp.sum(dq.astype(FULL), axis=0, keepdims=True)
            sum_v = sum_v + jnp.sum(dv.astype(FULL), axis=0, keepdims=True)
        for h in range(4):
            dsum[pl.ds(t * 4 + h, 128, stride=16), :] = sums[h]
        at = pl.ds(pl.multiple_of(t * 128, 128), 128)
        small[6:7, at] = sum_q
        small[7:8, at] = sum_v
        grads[0, t, :, 0:384] = mm(n1_t[...], dqkv[t]).astype(LOW)
        return 0

    lax.fori_loop(0, 4, backward, 0)

    def last(k, _):
        rows = pl.ds(pl.multiple_of(k * 128, 128), 128)
        n = jnp.zeros((128, 512), FULL)
        for t in range(4):
            n = n + mm_nt(dqkv[t, rows, :], w[0, t, :, 0:384])
        x = x1[rows, :]
        gmid[rows, :] += norm_back(n, x, r1[rows, :], vec[0:1, :])
        small[0:1, 0:512] += jnp.sum(n * x, axis=0, keepdims=True)
        small[1:2, 0:512] += jnp.sum(n, axis=0, keepdims=True)
        return 0

    lax.fori_loop(0, 4, last, 0)
    lines = []
    for i in range(49):
        lines.append(three_lows(dsum[i * 16 : (i + 1) * 16, :] + dsum[(64 + i) * 16 : (65 + i) * 16, :]))
    total = mm_nt(jnp.concatenate(lines, axis=1), onehot[...])
    small[:, 512:768] = total[0:16] + total[16:32] + total[32:48]

    field[...] = jnp.zeros((4, 16, 512), FULL)
    for i in range(28):
        image, r = i // 14, i % 14
        top = (image * 4 + (r // 7) * 2) * 64 + (r % 7) * 7
        for side, (src, dst) in enumerate(((mid, block), (gmid, igrad))):
            page = field.at[(2 * i + side) % 4]
            page[0:7, :] = src[top : top + 7, :]
            page[7:14, :] = src[top + 64 : top + 71, :]
            dst[image, r] = page[...].astype(LOW)


def middle(images, cotangents, gw, gs, vec, idx, mine):
    vm = lambda *shape, dtype=FULL: pltpu.VMEM(shape, dtype)
    whole = pl.BlockSpec(memory_space=pltpu.VMEM)
    anywhere = pl.BlockSpec(memory_space=pl.ANY)
    return pl.pallas_call(
        functools.partial(middle_kernel, mine=mine),
        out_shape=(
            jax.ShapeDtypeStruct((3, 4, 512, 512), LOW),
            jax.ShapeDtypeStruct((2, 14, 16, 512), LOW),
            jax.ShapeDtypeStruct((2, 14, 16, 512), LOW),
            jax.ShapeDtypeStruct((16, 768), FULL),
        ),
        in_specs=[anywhere] * 3 + [whole] * 3,
        out_specs=[whole] * 4,
        scratch_shapes=[
            vm(2, 14, 14, 512, dtype=LOW), vm(2, 14, 14, 512, dtype=LOW), vm(3, 4, 512, 512, dtype=LOW),
            vm(512, 512), vm(512, 512), vm(512, 512, dtype=LOW), vm(512, 512, dtype=LOW),
            vm(512, 512, dtype=LOW), vm(512, 512, dtype=LOW), vm(512, 512), vm(512, 1),
            vm(512, 512, dtype=LOW), vm(512, 512, dtype=LOW), vm(512, 512), vm(512, 1),
            vm(4, 3, 512, 128, dtype=LOW), vm(4, 4, 4, 128, 128, dtype=LOW), vm(4, 512, 128, dtype=LOW),
            vm(512, 512), vm(4, 512, 512, dtype=LOW), vm(4, 512, 512, dtype=LOW),
            vm(512, 512), vm(512, 512, dtype=LOW), vm(512, 512, dtype=LOW), vm(4, 512, 384, dtype=LOW),
            vm(256, 49 * 128, dtype=LOW), vm(48, 49 * 128), vm(2048, 128), vm(2048, 128), vm(16, 256), vm(4, 16, 512),
            pltpu.SemaphoreType.DMA((5,)),
        ],
        compiler_params=pltpu.CompilerParams(vmem_limit_bytes=62 * 2**20),
        name="block_forward_backward",
    )(images, cotangents, gw, gs, vec, idx)


def wide_index(rel_index):
    edge = jnp.pad(rel_index, ((0, 7), (0, 15)), constant_values=-1)
    return jnp.concatenate([edge, edge], axis=1)


def block_dims(full):
    dims = []
    for axis, size in ((2, 2), (1, 4), (2, 2), (0, 4)):
        if axis in full:
            dims.append(size)
    return tuple(dims)


def each(dims, fn):
    outer = dims[:-1]
    count = 1
    for size in outer:
        count *= size
    if count == 1:
        fn(())
        return

    def body(n, _):
        index = []
        for size in reversed(outer):
            index.append(n % size)
            n = n // size
        fn(tuple(reversed(index)))
        return 0

    lax.fori_loop(0, count, body, 0)


def scatter_kernel(
    g_ref, block_ref, igrad_ref, small_ref,
    mine_ref, blocks_ref, igrads_ref, total_ref,
    sib, part, slot00, slot10, slot20, slot01, slot11, slot21, slot02, slot12, slot22, steps,
    local_sem, sib_out, sib_in, out_sem, in_sem, small_out, small_in, mate_out, mate_in,
):
    slots = ((slot00, slot01, slot02), (slot10, slot11, slot12), (slot20, slot21, slot22))
    place = Place()
    core, step = place.core, place.step
    t = lax.axis_index("tensor")
    other_z = (place.z // 2) * 2 + 1 - place.z % 2
    sibling = place.sibling()
    z_mate = place.device((place.x, place.y, other_z))
    across = place.device((place.x, place.y, other_z), 1 - core)
    barrier = pltpu.get_barrier_semaphore()
    partners = [place.along(axis, by) for axis in range(3) for by in (1, 2, 3)] + [sibling, across]
    for device in partners:
        pl.semaphore_signal(barrier, inc=1, device_id=device, device_id_type=MESH)
    pl.semaphore_wait(barrier, len(partners))

    sends = []

    def send(src, dst, out, into, device):
        copy = pltpu.make_async_remote_copy(src, dst, out, into, device, MESH)
        copy.start()
        sends.append(copy)

    def wait_in(block, out, into):
        pltpu.make_async_remote_copy(block, block, out, into, sibling, MESH).wait_recv()

    shifts = (2, -step, step, 0)
    for k in range(4):
        for p in range(3):
            axis = ORDERS[p][2]
            full = ORDERS[p][:2]
            shift = (2, step, -step, 0)[k]
            src = block_of(g_ref, (p,), place, 1 - core, full, axis, shift)
            dst = block_of(sib, (p,), place, None, full, axis, shift)
            send(src, dst, sib_out.at[p, k], sib_in.at[p, k], sibling)
    own = []
    for p in range(3):
        copy = pltpu.make_async_copy(g_ref.at[p, :, core], part.at[p], local_sem.at[p])
        copy.start()
        own.append(copy)
    outs = ((block_ref, blocks_ref), (igrad_ref, igrads_ref))
    rows = pl.ds(t * 2, 2)
    for n, (src, dst) in enumerate(outs):
        copy = pltpu.make_async_copy(src, dst.at[rows], local_sem.at[3 + n])
        copy.start()
        own.append(copy)
        send(src, dst.at[rows], mate_out.at[n, 0], mate_in.at[n, 0], z_mate)
        send(src, dst.at[rows], mate_out.at[n, 1], mate_in.at[n, 1], sibling)

    def small_start(k):
        if k < 3:
            at = place.at[k]
            for shift in (1, 2, 3):
                send(
                    steps.at[k, at], steps.at[k, at], small_out.at[k, shift - 1], small_in.at[k, shift - 1],
                    place.along(k, shift),
                )
        else:
            send(steps.at[3, core], steps.at[3, core], small_out.at[3, 0], small_in.at[3, 0], sibling)

    def small_finish(k):
        if k < 3:
            for shift in (1, 2, 3):
                at = (place.at[k] - shift + 4) % 4
                wait_in(steps.at[k, at], small_out.at[k, shift - 1], small_in.at[k, shift - 1])
            return (steps[k, 0] + steps[k, 1]) + (steps[k, 2] + steps[k, 3])
        wait_in(steps.at[3, 1 - core], small_out.at[3, 0], small_in.at[3, 0])
        return steps[3, 0] + steps[3, 1]

    def small_next(k):
        value = small_finish(k)
        steps[k + 1, place.at[k + 1] if k < 2 else core] = value
        small_start(k + 1)

    steps[0, place.x] = small_ref[...]
    small_start(0)
    for p in range(3):
        own[p].wait()

    def add_sibling(p, k):
        axis, full = ORDERS[p][2], ORDERS[p][:2]
        there = block_of(sib, (p,), place, None, full, axis, shifts[k])
        here = block_of(part, (p,), place, None, full, axis, shifts[k])
        wait_in(there, sib_out.at[p, k], sib_in.at[p, k])

        def add(index):
            here[index] = here[index] + there[index]

        each(block_dims(full), add)

    def wait_slot(p, phase, kind):
        slot = slots[p][phase].at[kind]
        wait_in(slot, out_sem.at[p, phase, kind], in_sem.at[p, phase, kind])
        return slot

    for phase in range(3):
        rank = 2 - phase
        for k, shift, kind, toward in ((0, 2, 0, step), (1, -step, 2, -step)):
            for p in range(3):
                axis, full = ORDERS[p][rank], ORDERS[p][:rank]
                if phase == 0:
                    add_sibling(p, k)
                send(
                    block_of(part, (p,), place, None, full, axis, shift), slots[p][phase].at[kind],
                    out_sem.at[p, phase, kind], in_sem.at[p, phase, kind], place.along(axis, toward),
                )
        if phase == 0:
            for p in range(3):
                add_sibling(p, 2)
            small_next(0)
        if phase == 1:
            small_next(2)
        for p in range(3):
            axis, full = ORDERS[p][rank], ORDERS[p][:rank]
            slot = wait_slot(p, phase, 0)
            near = block_of(part, (p,), place, None, full, axis, step)

            def add(index):
                near[index] = near[index] + slot[index]

            each(block_dims(full) or (1,), add)
            send(
                near, slots[p][phase].at[1],
                out_sem.at[p, phase, 1], in_sem.at[p, phase, 1], place.along(axis, step),
            )
        if phase == 0:
            for p in range(3):
                add_sibling(p, 3)
            small_next(1)
        for p in range(3):
            axis, full = ORDERS[p][rank], ORDERS[p][:rank]
            one = wait_slot(p, phase, 2)
            two = wait_slot(p, phase, 1)
            here = block_of(part, (p,), place, None, full, axis, 0)
            if phase == 2:
                mine_ref[p] = here[...].astype(FULL) + one[...].astype(FULL) + two[...].astype(FULL)
            else:
                def add_both(index):
                    total = here[index].astype(FULL) + one[index].astype(FULL) + two[index].astype(FULL)
                    here[index] = total.astype(LOW)

                each(block_dims(full), add_both)
    total_ref[...] = small_finish(3)
    mate = place.z % 2
    their = pl.ds(((1 - mate) * 2 + core) * 2, 2)
    for n, (src, dst) in enumerate(outs):
        wait_in(dst.at[their], mate_out.at[n, 0], mate_in.at[n, 0])
        send(dst.at[their], dst.at[their], mate_out.at[n, 2], mate_in.at[n, 2], sibling)
    for n, (src, dst) in enumerate(outs):
        wait_in(dst.at[pl.ds((mate * 2 + 1 - core) * 2, 2)], mate_out.at[n, 1], mate_in.at[n, 1])
        wait_in(dst.at[pl.ds(((1 - mate) * 2 + 1 - core) * 2, 2)], mate_out.at[n, 2], mate_in.at[n, 2])
    for copy in own[3:]:
        copy.wait()
    for copy in sends:
        copy.wait_send()


def scatter(g, block, igrad, small):
    anywhere = pl.BlockSpec(memory_space=pl.ANY)
    whole = pl.BlockSpec(memory_space=pltpu.VMEM)
    slot_shapes = [
        pltpu.VMEM((3, *block_dims(ORDERS[p][: 2 - phase]), 16, 512), LOW) for phase in range(3) for p in range(3)
    ]
    return pl.pallas_call(
        scatter_kernel,
        out_shape=(
            jax.ShapeDtypeStruct((3, 16, 512), FULL),
            jax.ShapeDtypeStruct((8, 14, 16, 512), LOW),
            jax.ShapeDtypeStruct((8, 14, 16, 512), LOW),
            jax.ShapeDtypeStruct((16, 768), FULL),
        ),
        in_specs=[anywhere, anywhere, anywhere, whole],
        out_specs=[whole, anywhere, anywhere, whole],
        scratch_shapes=[
            pltpu.VMEM((3, 2, 4, 2, 4, 16, 512), LOW),
            pltpu.VMEM((3, 2, 4, 2, 4, 16, 512), LOW),
            *slot_shapes,
            pltpu.VMEM((4, 4, 16, 768), FULL),
            pltpu.SemaphoreType.DMA((5,)),
            pltpu.SemaphoreType.DMA((3, 4)),
            pltpu.SemaphoreType.DMA((3, 4)),
            pltpu.SemaphoreType.DMA((3, 3, 3)),
            pltpu.SemaphoreType.DMA((3, 3, 3)),
            pltpu.SemaphoreType.DMA((4, 3)),
            pltpu.SemaphoreType.DMA((4, 3)),
            pltpu.SemaphoreType.DMA((2, 3)),
            pltpu.SemaphoreType.DMA((2, 3)),
        ],
        compiler_params=pltpu.CompilerParams(
            collective_id=1, has_side_effects=True, vmem_limit_bytes=40 * 2**20
        ),
        name="scatter_gradients",
    )(g, block, igrad, small)


STEP = 10
REL = 169
BETA_ONE = 0.9
BETA_TWO = 0.999
ADAM_EPS = 1e-08
RATE_MATRIX = 0.1
RATE_VECTOR = 0.2
RATE_TABLE = 0.5
WEIGHT_DECAY = 0.05


def adam_step(weight, grad, first, second, rate, decay):
    first_new = BETA_ONE * first + (1.0 - BETA_ONE) * grad
    second_new = BETA_TWO * second + (1.0 - BETA_TWO) * grad * grad
    first_hat = first_new / (1.0 - BETA_ONE**STEP)
    second_hat = second_new / (1.0 - BETA_TWO**STEP)
    updated = weight - rate * (first_hat / (jnp.sqrt(second_hat) + ADAM_EPS) + decay * weight)
    return (updated, first_new, second_new)


def on_device(
    images,
    out_grad,
    rel_index,
    attn_weight,
    attn_first,
    attn_second,
    proj_weight,
    proj_first,
    proj_second,
    up_weight,
    up_first,
    up_second,
    down_weight,
    down_first,
    down_second,
    vectors,
    vec_first,
    vec_second,
    head_bias,
    head_first,
    head_second,
    unit_bias,
    unit_first,
    unit_second,
    rel_table,
    table_first,
    table_second,
):
    t = lax.axis_index("tensor")
    shards = jnp.stack(
        [
            jnp.concatenate([attn_weight.reshape(16, 384), proj_weight.T], axis=1),
            up_weight,
            down_weight.T,
        ]
    ).astype(LOW)
    lines = jnp.pad(rel_table.T, ((0, 0), (0, 256 - REL)))
    small_in = jnp.concatenate(
        [lines[:, :128], lines[:, 128:], head_bias, unit_bias.reshape(4, 128), jnp.zeros((2, 128), FULL)], axis=0
    )
    weights, smalls = gather(shards, small_in)
    grads, block, igrad, small = middle(
        images, out_grad, weights.reshape(3, 4, 512, 512), smalls, vectors, wide_index(rel_index),
        lambda: lax.axis_index("tensor") * 2,
    )
    mine, blocks, igrads, total = scatter(grads.reshape(3, 2, 2, 4, 2, 4, 16, 512), block, igrad, small)
    block_out = blocks[:, :, :14]
    images_grad = igrads[:, :, :14].astype(FULL)
    vec_grad = total[0:6, :512]
    head_grad = lax.dynamic_slice(total, (6, t * 128), (2, 128))
    unit_grad = lax.dynamic_slice(total, (8 + t, 0), (1, 512)).reshape(512)
    table_grad = lax.dynamic_slice(total, (t * 4, 512), (4, REL)).T
    attn_grad = mine[0, :, :384].reshape(16, 3, 128)
    proj_grad = mine[0, :, 384:].T
    up_grad = mine[1]
    down_grad = mine[2].T
    attn_out = adam_step(attn_weight, attn_grad, attn_first, attn_second, RATE_MATRIX, WEIGHT_DECAY)
    proj_out = adam_step(proj_weight, proj_grad, proj_first, proj_second, RATE_MATRIX, WEIGHT_DECAY)
    up_out = adam_step(up_weight, up_grad, up_first, up_second, RATE_MATRIX, WEIGHT_DECAY)
    down_out = adam_step(down_weight, down_grad, down_first, down_second, RATE_MATRIX, WEIGHT_DECAY)
    vec_out = adam_step(vectors, vec_grad, vec_first, vec_second, RATE_VECTOR, 0.0)
    head_out = adam_step(head_bias, head_grad, head_first, head_second, RATE_VECTOR, 0.0)
    unit_out = adam_step(unit_bias, unit_grad, unit_first, unit_second, RATE_VECTOR, 0.0)
    table_out = adam_step(rel_table, table_grad, table_first, table_second, RATE_TABLE, 0.0)
    return (
        (block_out, images_grad)
        + attn_out
        + proj_out
        + up_out
        + down_out
        + vec_out
        + head_out
        + unit_out
        + table_out
    )


def solution(mesh):
    in_specs = (
        P("fsdp", None, None, None),
        P("fsdp", None, None, None),
        P(),
        P("fsdp", None, "tensor"),
        P("fsdp", None, "tensor"),
        P("fsdp", None, "tensor"),
        P("tensor", "fsdp"),
        P("tensor", "fsdp"),
        P("tensor", "fsdp"),
        P("fsdp", "tensor"),
        P("fsdp", "tensor"),
        P("fsdp", "tensor"),
        P("tensor", "fsdp"),
        P("tensor", "fsdp"),
        P("tensor", "fsdp"),
        P(),
        P(),
        P(),
        P(None, "tensor"),
        P(None, "tensor"),
        P(None, "tensor"),
        P("tensor"),
        P("tensor"),
        P("tensor"),
        P(None, "tensor"),
        P(None, "tensor"),
        P(None, "tensor"),
    )
    out_specs = (
        P("fsdp", None, None, None),
        P("fsdp", None, None, None),
        P("fsdp", None, "tensor"),
        P("fsdp", None, "tensor"),
        P("fsdp", None, "tensor"),
        P("tensor", "fsdp"),
        P("tensor", "fsdp"),
        P("tensor", "fsdp"),
        P("fsdp", "tensor"),
        P("fsdp", "tensor"),
        P("fsdp", "tensor"),
        P("tensor", "fsdp"),
        P("tensor", "fsdp"),
        P("tensor", "fsdp"),
        P(),
        P(),
        P(),
        P(None, "tensor"),
        P(None, "tensor"),
        P(None, "tensor"),
        P("tensor"),
        P("tensor"),
        P("tensor"),
        P(None, "tensor"),
        P(None, "tensor"),
        P(None, "tensor"),
    )
    return jax.shard_map(
        on_device, mesh=mesh, in_specs=in_specs, out_specs=out_specs, check_vma=False
    )
```

```python
import types

import jax
import jax.numpy as jnp
from jax import lax
from jax.experimental import pallas as pl
from jax.experimental.pallas import tpu as pltpu
from jax.sharding import PartitionSpec as P

MESH = pl.DeviceIdType.MESH
LOW = jnp.bfloat16
FULL = jnp.float32
EPS = 1e-5
SCALE = 32.0 ** -0.5
BLOCKED = -1e30
STEP = 10
REL = 169
BETA_ONE = 0.9
BETA_TWO = 0.999
ADAM_EPS = 1e-08
RATE_MATRIX = 0.1
RATE_VECTOR = 0.2
RATE_TABLE = 0.5
WEIGHT_DECAY = 0.05
ORDERS = ((0, 1, 2), (1, 2, 0), (2, 0, 1))
SUMS = (((0, 1, 2), (1, 0, 2), (1, 0, 2)), ((0, 1, 2), (1, 0, 2), (0, 1, 2)))
WIDTHS = (128, 384)


class Place:
    def __init__(self):
        f = lax.axis_index("fsdp")
        self.t = lax.axis_index("tensor")
        x, y = f % 4, f // 8
        z = ((f // 4) % 2) * 2 + self.t // 2
        self.core = self.t % 2
        self.at = (x, y, z)
        mate = (x, y, (z // 2) * 2 + 1 - z % 2)
        self.sibling = self.device(core=1 - self.core)
        self.z_mate = self.device(mate)
        self.across = self.device(mate, 1 - self.core)
        self.mate_t = (1 - z % 2) * 2 + self.core

    def device(self, at=None, core=None):
        x, y, z = self.at if at is None else at
        core = self.core if core is None else core
        return (y * 8 + (z // 2) * 4 + x, (z % 2) * 2 + core)

    def along(self, axis, by):
        at = list(self.at)
        at[axis] = (at[axis] + by + 4) % 4
        return self.device(at)


def block_of(ref, lead, place, core, full, axis=None, shift=0):
    whole = slice(None)
    at = list(place.at)
    if axis is not None:
        at[axis] = (at[axis] + shift + 4) % 4
    x, y, z = at
    x = whole if 0 in full else x
    y = whole if 1 in full else y
    low, high = (whole, whole) if 2 in full else (z % 2, z // 2)
    return ref.at[(*lead, low, core, y, high, x)] if core is not None else ref.at[(*lead, low, y, high, x)]


def block_dims(full):
    return tuple(size for axis, size in ((2, 2), (1, 4), (2, 2), (0, 4)) if axis in full)


def each(dims, fn):
    outer = dims[:-1]
    count = 1
    for size in outer:
        count *= size
    if count == 1:
        fn((0,) * len(outer))
        return

    def body(n, _):
        index = []
        for size in reversed(outer):
            index.append(n % size)
            n = n // size
        fn(tuple(reversed(index)))
        return 0

    lax.fori_loop(0, count, body, 0)


def mm(a, b):
    return lax.dot_general(a, b, (((1,), (0,)), ((), ())), preferred_element_type=FULL)


def mm_nt(a, b):
    return lax.dot_general(a, b, (((1,), (1,)), ((), ())), preferred_element_type=FULL)


def mm_tn(a, b):
    return lax.dot_general(a, b, (((0,), (0,)), ((), ())), preferred_element_type=FULL)


def three_lows(a):
    high = a.astype(LOW)
    rest = a - high.astype(FULL)
    middle = rest.astype(LOW)
    last = (rest - middle.astype(FULL)).astype(LOW)
    return jnp.concatenate([high, middle, last], axis=0)


def normed(v):
    center = v - jnp.mean(v, axis=-1, keepdims=True)
    r = lax.rsqrt(jnp.mean(center * center, axis=-1, keepdims=True) + EPS)
    return center * r, r


def norm_back(n, x, r, offset):
    q = n * (1.0 + offset)
    return r * (q - jnp.mean(q, axis=-1, keepdims=True) - x * jnp.mean(q * x, axis=-1, keepdims=True))


def gelu_parts(u):
    size = jnp.abs(u)
    k = 1.0 / (1.0 + (0.3275911 * 0.7071067811865476) * size)
    bell = jnp.exp(-0.5 * u * u)
    poly = k * (0.254829592 + k * (-0.284496736 + k * (1.421413741 + k * (-1.453152027 + k * 1.061405429))))
    tail = 0.5 * poly * bell
    share = jnp.where(u < 0, tail, 1.0 - tail)
    return u * share, share + u * bell * 0.3989422804014327


def lane_mask(h):
    lane = lax.broadcasted_iota(jnp.int32, (128, 128), 1)
    return (lane >= h * 32) & (lane < h * 32 + 32)


def keep(mask, a):
    return jnp.where(mask, a, jnp.zeros_like(a))


def spans():
    for image in range(2):
        for r in range(14):
            for side in range(2):
                window = image * 4 + (r // 7) * 2 + side
                yield image, r * 14 + side * 7, window * 64 + (r % 7) * 7


def block_kernel(ref):
    images, cotangents, vec, idx = ref.images, ref.cotangents, ref.vec, ref.idx
    w = (ref.w1, ref.w2)
    g = (ref.g1, ref.g2)
    sib = (ref.sib1, ref.sib2)
    gs, small, steps = ref.gs, ref.small, ref.steps
    tok, cot, cot_low, cot_t = ref.tok, ref.cot, ref.cot_low, ref.cot_t
    n1, n1_t, x1, r1 = ref.n1, ref.n1_t, ref.x1, ref.r1
    n2, n2_t, x2, r2 = ref.n2, ref.n2_t, ref.x2, ref.r2
    qkv, probs, att, mid, hid, gpre = ref.qkv, ref.probs, ref.att, ref.mid, ref.hid, ref.gpre
    gmid, gml, gml_t, dqkv = ref.gmid, ref.gml, ref.gml_t, ref.dqkv
    onehot, spread, bias, dsum, table = ref.onehot, ref.spread, ref.bias, ref.dsum, ref.table
    stage, field, outs = ref.stage, ref.field, ref.outs
    local = ref.local_sem

    place = Place()
    t_own, core = place.t, place.core
    barrier = pltpu.get_barrier_semaphore()
    partners = [place.along(axis, by) for axis in range(3) for by in (1, 2, 3)] + [place.sibling, place.across]
    for device in partners:
        pl.semaphore_signal(barrier, inc=1, device_id=device, device_id_type=MESH)

    copies_in = [
        pltpu.make_async_copy(images, ref.img, local.at[0]),
        pltpu.make_async_copy(cotangents, ref.cimg, local.at[1]),
    ]
    for copy in copies_in:
        copy.start()

    sends = []

    def send(src, dst, out, into, device):
        copy = pltpu.make_async_remote_copy(src, dst, out, into, device, MESH)
        copy.start()
        sends.append(copy)

    def wait_in(block, out, into):
        pltpu.make_async_remote_copy(block, block, out, into, place.sibling, MESH).wait_recv()

    x, y, z = place.at
    own = (z % 2, core, y, z // 2, x)
    for p in range(3):
        w[0][(p, *own)] = ref.attn[p].astype(LOW)
    proj, up, down = ref.proj[...].astype(LOW), ref.up[...].astype(LOW), ref.down[...].astype(LOW)
    w[1][(0, *own)] = jnp.concatenate([proj, up[:, 0:256]], axis=1)
    w[1][(1, *own)] = jnp.concatenate([up[:, 256:512], down[:, 0:128]], axis=1)
    w[1][(2, *own)] = down[:, 128:512]
    mine = gs.at[t_own]
    mine[...] = jnp.zeros((16, 128), FULL)
    mine[0:4, :] = ref.rel[:, 0:128]
    mine[4:8, 0 : REL - 128] = ref.rel[:, 128:REL]
    mine[8:10, :] = ref.head[...]
    for k in range(4):
        mine[10 + k : 11 + k, :] = ref.unit[:, k * 128 : (k + 1) * 128]

    pl.semaphore_wait(barrier, len(partners))

    in_sem, out_sem, sib_in, sib_out = ref.w_in, ref.w_out, ref.ws_in, ref.ws_out

    def gather_start(b, phase):
        for p in range(3):
            axis, done = ORDERS[p][phase], ORDERS[p][:phase]
            block = block_of(w[b], (p,), place, core, done)
            for shift in (1, 3, 2):
                at = (b, p, phase, shift - 1)
                send(block, block, out_sem.at[at], in_sem.at[at], place.along(axis, shift))
            if phase == 2:
                send(block, block, sib_out.at[b, p, 0], sib_in.at[b, p, 0], place.sibling)

    def gather_finish(b, phase, shifts=(1, 3, 2)):
        for shift in shifts:
            for p in range(3):
                axis, done = ORDERS[p][phase], ORDERS[p][:phase]
                block = block_of(w[b], (p,), place, core, done, axis, -shift)
                at = (b, p, phase, shift - 1)
                wait_in(block, out_sem.at[at], in_sem.at[at])
                if phase == 2:
                    send(block, block, sib_out.at[b, p, shift], sib_in.at[b, p, shift], place.sibling)

    def gather_last(b):
        for p in range(3):
            axis, done = ORDERS[p][2], ORDERS[p][:2]
            for shift in range(4):
                block = block_of(w[b], (p,), place, 1 - core, done, axis, -shift)
                wait_in(block, sib_out.at[b, p, shift], sib_in.at[b, p, shift])

    mates = (place.sibling, place.z_mate, place.across)
    mate_ts = (t_own + 1 - 2 * core, place.mate_t, (1 - z % 2) * 2 + 1 - core)
    gather_start(0, 0)
    gather_start(1, 0)
    for k in range(3):
        send(mine, mine, ref.s_out.at[k], ref.s_in.at[k], mates[k])

    wide = ref.wide
    wide[...] = jnp.full((56, 128), -1, jnp.int32)
    wide[0:49, 0:49] = idx[...]
    wide[0:49, 64:113] = idx[...]
    row_id = lax.broadcasted_iota(jnp.int32, (256, 128), 0)
    for i in range(49):
        onehot[:, i * 128 : (i + 1) * 128] = (row_id == wide[i : i + 1, :]).astype(FULL).astype(LOW)
    small[...] = jnp.zeros((16, 768), FULL)
    tok[...] = jnp.zeros((512, 512), FULL)
    cot[...] = jnp.zeros((512, 512), FULL)
    gather_finish(0, 0)
    gather_start(0, 1)
    gather_finish(1, 0)
    gather_start(1, 1)
    for n, (source, copy, dst) in enumerate(zip((ref.img, ref.cimg), copies_in, (tok, cot))):
        copy.wait()
        if n == 1:
            gather_finish(0, 1)
            gather_start(0, 2)

        def widen(k, _):
            rows = pl.ds(pl.multiple_of(k * 112, 112), 112)
            for k4 in range(4):
                stage[k4, rows, :] = source[rows, k4 * 128 : (k4 + 1) * 128].astype(FULL)
            return 0

        lax.fori_loop(0, 14, widen, 0)
        for image, first, top in spans():
            for k in range(4):
                dst[top : top + 7, k * 128 : (k + 1) * 128] = stage[
                    k, pl.ds(first * 8 + image + 2 * t_own, 7, stride=8), :
                ]
    gather_finish(1, 1)

    def start(k, _):
        rows = pl.ds(pl.multiple_of(k * 64, 64), 64)
        xs, r = normed(tok[rows, :])
        x1[rows, :] = xs
        r1[rows, :] = r
        n1[rows, :] = (xs * (1.0 + vec[0:1, :]) + vec[1:2, :]).astype(LOW)
        c = cot[rows, :]
        cot_low[rows, :] = c.astype(LOW)
        small[5:6, 0:512] += jnp.sum(c, axis=0, keepdims=True)
        return 0

    lax.fori_loop(0, 8, start, 0)
    for k in range(3):
        wait_in(gs.at[mate_ts[k]], ref.s_out.at[k], ref.s_in.at[k])
    for t in range(4):
        table[t * 4 : t * 4 + 4, 0:128] = gs[t, 0:4, :]
        table[t * 4 : t * 4 + 4, 128:256] = gs[t, 4:8, :]
    spread[...] = mm(three_lows(table[...]), onehot[...])
    lane = lax.broadcasted_iota(jnp.int32, (16, 128), 1)
    low_side = lane < 49
    high_side = (lane >= 64) & (lane < 113)
    for i in range(64):
        if i < 49:
            at = slice(i * 128, (i + 1) * 128)
            line = spread[0:16, at] + spread[16:32, at] + spread[32:48, at]
        else:
            line = jnp.zeros((16, 128), FULL)
        bias[i * 16 : (i + 1) * 16, :] = jnp.where(low_side, line, BLOCKED)
        bias[(64 + i) * 16 : (65 + i) * 16, :] = jnp.where(high_side, line, BLOCKED)
    gather_finish(0, 2, (1, 3))
    gather_start(1, 2)
    n1_t[...] = n1[...].T
    cot_t[...] = cot_low[...].T
    gather_finish(0, 2, (2,))
    gather_last(0)

    def columns(b, p, t, a, z):
        return w[b][p, t // 2, t % 2, :, :, :, :, a:z].reshape(512, z - a)

    def w_qkv(t):
        return jnp.concatenate([columns(0, c, t, 0, 128) for c in range(3)], axis=1)

    def w_proj(t):
        return columns(1, 0, t, 0, 128)

    def w_up(t):
        return jnp.concatenate([columns(1, 0, t, 128, 384), columns(1, 1, t, 0, 256)], axis=1)

    def w_down(t):
        return jnp.concatenate([columns(1, 1, t, 256, 384), columns(1, 2, t, 0, 384)], axis=1)

    def put_grad(b, p, t, a, value):
        g[b][p, t // 2, t % 2, :, :, :, :, a : a + value.shape[1]] = value.astype(LOW).reshape(
            4, 2, 4, 16, value.shape[1]
        )

    def forward(t, _):
        mixed = mm(n1[...], w_qkv(t))
        q_bias, v_bias = gs[t, 8:9, :], gs[t, 9:10, :]
        qkv[t, 0] = (mixed[:, 0:128] + q_bias).astype(LOW)
        qkv[t, 1] = mixed[:, 128:256].astype(LOW)
        qkv[t, 2] = (mixed[:, 256:384] + v_bias).astype(LOW)
        for wp in range(4):
            rows = slice(wp * 128, (wp + 1) * 128)
            q, k, v = qkv[t, 0, rows], qkv[t, 1, rows], qkv[t, 2, rows]
            ps, vs = [], []
            for h in range(4):
                mask = lane_mask(h)
                s = mm_nt(keep(mask, q), k) * SCALE + bias[pl.ds(t * 4 + h, 128, stride=16), :]
                e = jnp.exp(s - jnp.max(s, axis=-1, keepdims=True))
                p = (e / jnp.sum(e, axis=-1, keepdims=True)).astype(LOW)
                probs[t, wp, h] = p
                ps.append(p)
                vs.append(keep(mask, v))
            att[t, rows] = mm(jnp.concatenate(ps, axis=1), jnp.concatenate(vs, axis=0)).astype(LOW)
        return 0

    lax.fori_loop(0, 3, forward, 0)
    gather_finish(1, 2, (1, 3))
    lax.fori_loop(3, 4, forward, 0)
    gather_finish(1, 2, (2,))
    gather_last(1)

    def second(k, _):
        rows = pl.ds(pl.multiple_of(k * 128, 128), 128)
        acc = tok[rows, :] + vec[2:3, :]
        for t in range(4):
            acc = acc + mm_nt(att[t, rows, :], w_proj(t))
        mid[rows, :] = acc
        xs, r = normed(acc)
        x2[rows, :] = xs
        r2[rows, :] = r
        n2[rows, :] = (xs * (1.0 + vec[3:4, :]) + vec[4:5, :]).astype(LOW)
        return 0

    lax.fori_loop(0, 4, second, 0)
    n2_t[...] = n2[...].T

    def feed(t, _):
        unit = jnp.concatenate([gs[t, 10 + k : 11 + k, :] for k in range(4)], axis=1)
        up_t, down_t = w_up(t), w_down(t)

        def rows_of(k, total):
            rows = pl.ds(pl.multiple_of(k * 128, 128), 128)
            pre = mm(n2[rows, :], up_t) + unit
            value, slope = gelu_parts(pre)
            hid[t, rows, :] = value.astype(LOW)
            grad = mm(cot_low[rows, :], down_t) * slope
            gpre[t, rows, :] = grad.astype(LOW)
            return total + jnp.sum(grad, axis=0, keepdims=True)

        small[pl.ds(8 + t, 1), 0:512] = lax.fori_loop(0, 4, rows_of, jnp.zeros((1, 512), FULL))
        grad_up = mm(n2_t[...], gpre[t])
        put_grad(1, 0, t, 128, grad_up[:, 0:256])
        put_grad(1, 1, t, 0, grad_up[:, 256:512])
        grad_down = mm(cot_t[...], hid[t])
        put_grad(1, 1, t, 256, grad_down[:, 0:128])
        put_grad(1, 2, t, 0, grad_down[:, 128:512])
        return 0

    lax.fori_loop(0, 4, feed, 0)

    g_in, g_out, gs_in, gs_out = ref.g_in, ref.g_out, ref.gs_in, ref.gs_out
    slot = ref.slots

    def sum_core(b, p):
        axis, full = SUMS[b][p][0], SUMS[b][p][1:]
        for shift in (1, 3, 2, 0):
            src = block_of(g[b], (p,), place, 1 - core, full, axis, shift)
            dst = block_of(sib[b], (p,), place, None, full, axis, shift)
            send(src, dst, gs_out.at[b, p, shift], gs_in.at[b, p, shift], place.sibling)

    def sum_start(b, p, phase):
        axis, full = SUMS[b][p][phase], SUMS[b][p][phase + 1 :]
        for shift in (1, 3, 2, 0):
            here = block_of(g[b], (p,), place, core, full, axis, shift)
            if phase == 0:
                there = block_of(sib[b], (p,), place, None, full, axis, shift)
                wait_in(there, gs_out.at[b, p, shift], gs_in.at[b, p, shift])

                def add(index):
                    here[index] = here[index] + there[index]

                each(block_dims(full), add)
            if shift:
                at = (b, p, phase, shift - 1)
                send(here, slot[b, p, phase].at[shift - 1], g_out.at[at], g_in.at[at], place.along(axis, shift))

    def sum_finish(b, p, phase):
        axis, full = SUMS[b][p][phase], SUMS[b][p][phase + 1 :]
        here = block_of(g[b], (p,), place, core, full)
        came = [slot[b, p, phase].at[k] for k in range(3)]
        for k in range(3):
            wait_in(came[k], g_out.at[b, p, phase, k], g_in.at[b, p, phase, k])

        def total(index):
            one, two, three = (c[index].astype(FULL) for c in came)
            return (here[index].astype(FULL) + one) + (two + three)

        if phase == 2:
            return total(())

        def add(index):
            here[index] = total(index).astype(LOW)

        each(block_dims(full), add)
        return None

    sum_core(1, 1)
    sum_core(1, 2)

    def third(k, _):
        rows = pl.ds(pl.multiple_of(k * 128, 128), 128)
        out = mid[rows, :] + vec[5:6, :]
        n = jnp.zeros((128, 512), FULL)
        for t in range(4):
            out = out + mm_nt(hid[t, rows, :], w_down(t))
            n = n + mm_nt(gpre[t, rows, :], w_up(t))
        mid[rows, :] = out
        xs = x2[rows, :]
        grad = cot[rows, :] + norm_back(n, xs, r2[rows, :], vec[3:4, :])
        gmid[rows, :] = grad
        gml[rows, :] = grad.astype(LOW)
        small[2:3, 0:512] += jnp.sum(grad, axis=0, keepdims=True)
        small[3:4, 0:512] += jnp.sum(n * xs, axis=0, keepdims=True)
        small[4:5, 0:512] += jnp.sum(n, axis=0, keepdims=True)
        return 0

    lax.fori_loop(0, 4, third, 0)
    gml_t[...] = gml[...].T

    def proj_grad(t, _):
        put_grad(1, 0, t, 0, mm(gml_t[...], att[t]))
        return 0

    lax.fori_loop(0, 4, proj_grad, 0)
    sum_core(1, 0)

    o_in, o_out = ref.o_in, ref.o_out

    def give(n, half, src):
        rows = pl.ds(half * 208, 208)
        for image, first, top in spans():
            if image == half:
                field[half * 208 + first : half * 208 + first + 7, :] = src[top : top + 7, :]
        outs[n, t_own, rows, :] = field[rows, :].astype(LOW)
        block = outs.at[n, t_own, rows]
        send(block, block, o_out.at[n, half, 1], o_in.at[n, half, 1], place.z_mate)
        send(block, block, o_out.at[n, half, 0], o_in.at[n, half, 0], place.sibling)

    def came(n, half, kind):
        t = mate_ts[kind]
        block = outs.at[n, t, pl.ds(half * 208, 208)]
        wait_in(block, o_out.at[n, half, kind], o_in.at[n, half, kind])
        if kind == 1:
            send(block, block, o_out.at[n, half, 2], o_in.at[n, half, 2], place.sibling)

    def take(n, half, t):
        field[0:208, :] = outs[n, t, half * 208 : half * 208 + 208, :].astype(FULL)
        for k in range(4):
            stage[k, pl.ds(2 * t + half, 196, stride=8), :] = field[0:196, k * 128 : (k + 1) * 128]

    def take_near(n):
        for half in range(2):
            take(n, half, t_own)
            came(n, half, 0)
            take(n, half, mate_ts[0])

    def take_far(n):
        for half in range(2):
            take(n, half, mate_ts[1])
        for half in range(2):
            came(n, half, 2)
            take(n, half, mate_ts[2])

    field[...] = jnp.zeros((416, 512), FULL)
    for p in (1, 2, 0):
        sum_start(1, p, 0)
    give(0, 0, mid)
    give(0, 1, mid)

    def backward(t, _):
        ga = mm(gml[...], w_proj(t)).astype(LOW)
        sums = [jnp.zeros((128, 128), FULL) for _ in range(4)]
        sum_q = jnp.zeros((1, 128), FULL)
        sum_v = jnp.zeros((1, 128), FULL)
        for wp in range(4):
            rows = slice(wp * 128, (wp + 1) * 128)
            q, k, v, grad = qkv[t, 0, rows], qkv[t, 1, rows], qkv[t, 2, rows], ga[rows]
            dss, ps, ks, qs, gg = [], [], [], [], []
            for h in range(4):
                mask = lane_mask(h)
                p_low = probs[t, wp, h]
                p = p_low.astype(FULL)
                gh = keep(mask, grad)
                dp = mm_nt(gh, v)
                ds = (p * (dp - jnp.sum(dp * p, axis=-1, keepdims=True))).astype(LOW)
                sums[h] = sums[h] + ds.astype(FULL)
                dss.append(ds)
                ps.append(p_low)
                ks.append(keep(mask, k))
                qs.append(keep(mask, q))
                gg.append(gh)
            dq = (mm(jnp.concatenate(dss, axis=1), jnp.concatenate(ks, axis=0)) * SCALE).astype(LOW)
            dk = (mm_tn(jnp.concatenate(dss, axis=0), jnp.concatenate(qs, axis=0)) * SCALE).astype(LOW)
            dv = mm_tn(jnp.concatenate(ps, axis=0), jnp.concatenate(gg, axis=0)).astype(LOW)
            dqkv[t, rows, 0:128] = dq
            dqkv[t, rows, 128:256] = dk
            dqkv[t, rows, 256:384] = dv
            sum_q = sum_q + jnp.sum(dq.astype(FULL), axis=0, keepdims=True)
            sum_v = sum_v + jnp.sum(dv.astype(FULL), axis=0, keepdims=True)
        for h in range(4):
            dsum[pl.ds(t * 4 + h, 128, stride=16), :] = sums[h]
        at = pl.ds(pl.multiple_of(t * 128, 128), 128)
        small[6:7, at] = sum_q
        small[7:8, at] = sum_v
        grad = mm(n1_t[...], dqkv[t])
        for c in range(3):
            put_grad(0, c, t, 0, grad[:, c * 128 : (c + 1) * 128])
        return 0

    lax.fori_loop(0, 4, backward, 0)
    for p in range(3):
        sum_core(0, p)
    lines = []
    for i in range(49):
        lines.append(three_lows(dsum[i * 16 : (i + 1) * 16, :] + dsum[(64 + i) * 16 : (65 + i) * 16, :]))
    table_sum = mm_nt(jnp.concatenate(lines, axis=1), onehot[...])
    small[:, 512:768] = table_sum[0:16] + table_sum[16:32] + table_sum[32:48]

    def last(k, _):
        rows = pl.ds(pl.multiple_of(k * 128, 128), 128)
        n = jnp.zeros((128, 512), FULL)
        for t in range(4):
            n = n + mm_nt(dqkv[t, rows, :], w_qkv(t))
        xs = x1[rows, :]
        gmid[rows, :] += norm_back(n, xs, r1[rows, :], vec[0:1, :])
        small[0:1, 0:512] += jnp.sum(n * xs, axis=0, keepdims=True)
        small[1:2, 0:512] += jnp.sum(n, axis=0, keepdims=True)
        return 0

    lax.fori_loop(0, 2, last, 0)
    give(1, 0, gmid)
    for p in range(3):
        sum_start(0, p, 0)
    lax.fori_loop(2, 4, last, 0)
    give(1, 1, gmid)

    n_in, n_out = ref.n_in, ref.n_out

    def small_start(k):
        if k < 3:
            block = steps.at[k, place.at[k]]
            for shift in (1, 3, 2):
                send(block, block, n_out.at[k, shift - 1], n_in.at[k, shift - 1], place.along(k, shift))
        else:
            block = steps.at[3, core]
            send(block, block, n_out.at[3, 0], n_in.at[3, 0], place.sibling)

    def small_finish(k):
        if k < 3:
            for shift in (1, 3, 2):
                at = (place.at[k] - shift + 4) % 4
                wait_in(steps.at[k, at], n_out.at[k, shift - 1], n_in.at[k, shift - 1])
            return (steps[k, 0] + steps[k, 1]) + (steps[k, 2] + steps[k, 3])
        wait_in(steps.at[3, 1 - core], n_out.at[3, 0], n_in.at[3, 0])
        return steps[3, 0] + steps[3, 1]

    def small_next(k):
        value = small_finish(k)
        steps[k + 1, place.at[k + 1] if k < 2 else core] = value
        small_start(k + 1)

    steps[0, place.at[0]] = small[...]
    small_start(0)
    for half in range(2):
        came(0, half, 1)
    take_near(0)
    for p in range(3):
        sum_finish(1, p, 0)
        sum_start(1, p, 1)
    for p in range(3):
        sum_finish(0, p, 0)
        sum_start(0, p, 1)
    small_next(0)
    take_far(0)

    def narrow(k, _):
        rows = pl.ds(pl.multiple_of(k * 112, 112), 112)
        for k4 in range(4):
            ref.block_out[rows, k4 * 128 : (k4 + 1) * 128] = stage[k4, rows, :].astype(LOW)
        return 0

    lax.fori_loop(0, 14, narrow, 0)
    for p in range(3):
        sum_finish(0, p, 1)
        sum_start(0, p, 2)
    small_next(1)
    for p in range(3):
        sum_finish(1, p, 1)
        sum_start(1, p, 2)
    take_near(1)
    for half in range(2):
        came(1, half, 1)
    for p in range(3):
        ref.attn_grad[p] = sum_finish(0, p, 2)
    small_next(2)
    first, second_, third_ = (sum_finish(1, p, 2) for p in range(3))
    ref.proj_grad[...] = first[:, 0:128]
    ref.up_grad[:, 0:256] = first[:, 128:384]
    ref.up_grad[:, 256:512] = second_[:, 0:256]
    ref.down_grad[:, 0:128] = second_[:, 256:384]
    ref.down_grad[:, 128:512] = third_
    take_far(1)
    ref.total[...] = small_finish(3)
    results = []
    for k in range(4):
        lanes = ref.images_grad.at[:, pl.ds(k * 128, 128)]
        results.append(pltpu.make_async_copy(stage.at[k], lanes, local.at[k]))
        results[k].start()
    for copy in sends:
        copy.wait_send()
    for copy in results:
        copy.wait()


def run_block(images, cotangents, vec, idx, attn, proj, up, down, rel, head, unit):
    whole = pl.BlockSpec(memory_space=pltpu.VMEM)
    anywhere = pl.BlockSpec(memory_space=pl.ANY)
    ins = dict(
        images=anywhere, cotangents=anywhere, vec=whole, idx=whole, attn=whole, proj=whole,
        up=whole, down=whole, rel=whole, head=whole, unit=whole,
    )
    results = dict(
        block_out=((1568, 512), LOW, whole),
        images_grad=((1568, 512), FULL, anywhere),
        attn_grad=((3, 16, 128), FULL, whole),
        proj_grad=((16, 128), FULL, whole),
        up_grad=((16, 512), FULL, whole),
        down_grad=((16, 512), FULL, whole),
        total=((16, 768), FULL, whole),
    )
    square = (512, 512)
    scratch = dict(
        img=pltpu.VMEM((1568, 512), LOW),
        cimg=pltpu.VMEM((1568, 512), LOW),
        w1=pltpu.VMEM((3, 2, 2, 4, 2, 4, 16, 128), LOW),
        w2=pltpu.VMEM((3, 2, 2, 4, 2, 4, 16, 384), LOW),
        g1=pltpu.VMEM((3, 2, 2, 4, 2, 4, 16, 128), LOW),
        g2=pltpu.VMEM((3, 2, 2, 4, 2, 4, 16, 384), LOW),
        sib1=pltpu.VMEM((3, 2, 4, 2, 4, 16, 128), LOW),
        sib2=pltpu.VMEM((3, 2, 4, 2, 4, 16, 384), LOW),
        gs=pltpu.VMEM((4, 16, 128), FULL),
        small=pltpu.VMEM((16, 768), FULL),
        steps=pltpu.VMEM((4, 4, 16, 768), FULL),
        qkv=pltpu.VMEM((4, 3, 512, 128), LOW),
        probs=pltpu.VMEM((4, 4, 4, 128, 128), LOW),
        att=pltpu.VMEM((4, 512, 128), LOW),
        hid=pltpu.VMEM((4, 512, 512), LOW),
        gpre=pltpu.VMEM((4, 512, 512), LOW),
        dqkv=pltpu.VMEM((4, 512, 384), LOW),
        onehot=pltpu.VMEM((256, 49 * 128), LOW),
        spread=pltpu.VMEM((48, 49 * 128), FULL),
        bias=pltpu.VMEM((2048, 128), FULL),
        dsum=pltpu.VMEM((2048, 128), FULL),
        table=pltpu.VMEM((16, 256), FULL),
        wide=pltpu.VMEM((56, 128), jnp.int32),
        stage=pltpu.VMEM((4, 1568, 128), FULL),
        field=pltpu.VMEM((416, 512), FULL),
        outs=pltpu.VMEM((2, 4, 416, 512), LOW),
        r1=pltpu.VMEM((512, 1), FULL),
        r2=pltpu.VMEM((512, 1), FULL),
    )
    full, low = pltpu.VMEM(square, FULL), pltpu.VMEM(square, LOW)
    scratch.update(tok=full, cot=full, x1=full, x2=full, mid=full, gmid=full)
    scratch.update(cot_low=low, cot_t=low, n1=low, n1_t=low, n2=low, n2_t=low, gml=low, gml_t=low)
    slots = {}
    for b in range(2):
        for p in range(3):
            for phase in range(3):
                slots[b, p, phase] = pltpu.VMEM((3, *block_dims(SUMS[b][p][phase + 1 :]), 16, WIDTHS[b]), LOW)
    sems = dict(
        local_sem=(4,), w_in=(2, 3, 3, 3), w_out=(2, 3, 3, 3), ws_in=(2, 3, 4), ws_out=(2, 3, 4),
        s_in=(3,), s_out=(3,), g_in=(2, 3, 3, 3), g_out=(2, 3, 3, 3), gs_in=(2, 3, 4), gs_out=(2, 3, 4),
        o_in=(2, 2, 3), o_out=(2, 2, 3), n_in=(4, 3), n_out=(4, 3),
    )
    for name, shape in sems.items():
        scratch[name] = pltpu.SemaphoreType.DMA(shape)
    names = [*ins, *results, *scratch]

    def kernel(*refs):
        named = dict(zip(names, refs))
        block_kernel(types.SimpleNamespace(**named, slots=dict(zip(slots, refs[len(names) :]))))

    return pl.pallas_call(
        kernel,
        out_shape=tuple(jax.ShapeDtypeStruct(shape, dtype) for shape, dtype, _ in results.values()),
        in_specs=list(ins.values()),
        out_specs=[spec for _, _, spec in results.values()],
        scratch_shapes=[*scratch.values(), *slots.values()],
        compiler_params=pltpu.CompilerParams(
            collective_id=0, has_side_effects=True, vmem_limit_bytes=63 * 2**20
        ),
        name="block_forward_backward",
    )(images, cotangents, vec, idx, attn, proj, up, down, rel, head, unit)


def adam_step(weight, grad, first, second, rate, decay):
    first_new = BETA_ONE * first + (1.0 - BETA_ONE) * grad
    second_new = BETA_TWO * second + (1.0 - BETA_TWO) * grad * grad
    first_hat = first_new / (1.0 - BETA_ONE**STEP)
    second_hat = second_new / (1.0 - BETA_TWO**STEP)
    updated = weight - rate * (first_hat / (jnp.sqrt(second_hat) + ADAM_EPS) + decay * weight)
    return (updated, first_new, second_new)


PARAMETERS = (
    ((3, 16, 128), RATE_MATRIX, WEIGHT_DECAY),
    ((16, 128), RATE_MATRIX, WEIGHT_DECAY),
    ((16, 512), RATE_MATRIX, WEIGHT_DECAY),
    ((16, 512), RATE_MATRIX, WEIGHT_DECAY),
    ((6, 512), RATE_VECTOR, 0.0),
    ((2, 128), RATE_VECTOR, 0.0),
    ((1, 512), RATE_VECTOR, 0.0),
    ((4, REL), RATE_TABLE, 0.0),
)


def update_kernel(*refs):
    refs = list(refs)

    def some(count):
        taken = refs[:count]
        del refs[:count]
        return taken

    results, grads, states = some(2), some(5), some(24)
    results_out, states_out = some(2), some(24)
    held, grads_in, states_in, states_new = some(2), some(5), some(24), some(24)
    sems_in, sems_out = refs
    arriving = []
    leaving = []
    for n, (source, page, target) in enumerate(zip(results, held, results_out)):
        for k in range(2):
            rows = pl.ds(k * 784, 784)
            at = 2 * n + k
            arriving.append(pltpu.make_async_copy(source.at[rows], page.at[rows], sems_in.at[29 + at]))
            leaving.append(pltpu.make_async_copy(page.at[rows], target.at[rows], sems_out.at[24 + at]))
    loads = [
        pltpu.make_async_copy(a, b, sems_in.at[n]) for n, (a, b) in enumerate(zip(grads + states, grads_in + states_in))
    ]
    for copy in loads + arriving:
        copy.start()
    for copy in loads:
        copy.wait()
    t = lax.axis_index("tensor")
    total = grads_in[4]

    def picked(pieces):
        value = pieces[3]
        for k in (2, 1, 0):
            value = jnp.where(t == k, pieces[k], value)
        return value

    small = (
        total[0:6, 0:512],
        picked([total[6:8, k * 128 : (k + 1) * 128] for k in range(4)]),
        picked([total[8 + k : 9 + k, 0:512] for k in range(4)]),
        picked([total[4 * k : 4 * k + 4, 512 : 512 + REL] for k in range(4)]),
    )
    for coming, going in zip(arriving, leaving):
        coming.wait()
        going.start()
    stores = []
    for n, (_, rate, decay) in enumerate(PARAMETERS):
        grad = grads_in[n][...] if n < 4 else small[n - 4]
        weight, first, second = (states_in[3 * n + k][...] for k in range(3))
        for k, value in enumerate(adam_step(weight, grad, first, second, rate, decay)):
            at = 3 * n + k
            states_new[at][...] = value
            copy = pltpu.make_async_copy(states_new[at], states_out[at], sems_out.at[at])
            copy.start()
            stores.append(copy)
    for copy in stores + leaving:
        copy.wait()


def update(results, grads, states):
    anywhere = pl.BlockSpec(memory_space=pl.ANY)
    shapes = [shape for shape, _, _ in PARAMETERS for _ in range(3)]
    inner = [pltpu.VMEM(shape, FULL) for shape in shapes]
    out_shape = [jax.ShapeDtypeStruct(a.shape, a.dtype) for a in results]
    out_shape += [jax.ShapeDtypeStruct(shape, FULL) for shape in shapes]
    return pl.pallas_call(
        update_kernel,
        out_shape=out_shape,
        in_specs=[anywhere] * 31,
        out_specs=[anywhere] * 26,
        scratch_shapes=[
            *[pltpu.VMEM(a.shape, a.dtype) for a in [*results, *grads]], *inner, *inner,
            pltpu.SemaphoreType.DMA((33,)), pltpu.SemaphoreType.DMA((28,)),
        ],
        compiler_params=pltpu.CompilerParams(vmem_limit_bytes=60 * 2**20),
        name="adam_update",
    )(*results, *grads, *states)


def on_device(
    images,
    out_grad,
    rel_index,
    attn_weight,
    attn_first,
    attn_second,
    proj_weight,
    proj_first,
    proj_second,
    up_weight,
    up_first,
    up_second,
    down_weight,
    down_first,
    down_second,
    vectors,
    vec_first,
    vec_second,
    head_bias,
    head_first,
    head_second,
    unit_bias,
    unit_first,
    unit_second,
    rel_table,
    table_first,
    table_second,
):
    def flat(field):
        return jnp.transpose(field, (1, 2, 0, 3)).reshape(1568, 512)

    def unflat(rows):
        return jnp.transpose(rows.reshape(14, 14, 8, 512), (2, 0, 1, 3))

    def turned(a):
        return jnp.transpose(a, (1, 0, 2))

    def row(a):
        return a.reshape(1, 512)

    def same(a):
        return a

    def flipped(a):
        return a.T

    ways = (turned, flipped, same, flipped, same, same, row, flipped)
    back = (turned, flipped, same, flipped, same, same, lambda a: a.reshape(512), flipped)
    groups = (
        (attn_weight, attn_first, attn_second),
        (proj_weight, proj_first, proj_second),
        (up_weight, up_first, up_second),
        (down_weight, down_first, down_second),
        (vectors, vec_first, vec_second),
        (head_bias, head_first, head_second),
        (unit_bias, unit_first, unit_second),
        (rel_table, table_first, table_second),
    )
    states = [way(a) for way, group in zip(ways, groups) for a in group]
    attn, proj, up, down, vec, head, unit, rel = states[::3]
    block, igrad, *grads = run_block(
        flat(images), flat(out_grad), vec, rel_index, attn, proj, up, down, rel, head, unit
    )
    block, igrad, *new = update((block, igrad), grads, states)
    news = [way(a) for way, at in zip(back, range(0, 24, 3)) for a in new[at : at + 3]]
    return (unflat(block), unflat(igrad), *news)


def solution(mesh):
    in_specs = (
        P("fsdp", None, None, None),
        P("fsdp", None, None, None),
        P(),
        P("fsdp", None, "tensor"),
        P("fsdp", None, "tensor"),
        P("fsdp", None, "tensor"),
        P("tensor", "fsdp"),
        P("tensor", "fsdp"),
        P("tensor", "fsdp"),
        P("fsdp", "tensor"),
        P("fsdp", "tensor"),
        P("fsdp", "tensor"),
        P("tensor", "fsdp"),
        P("tensor", "fsdp"),
        P("tensor", "fsdp"),
        P(),
        P(),
        P(),
        P(None, "tensor"),
        P(None, "tensor"),
        P(None, "tensor"),
        P("tensor"),
        P("tensor"),
        P("tensor"),
        P(None, "tensor"),
        P(None, "tensor"),
        P(None, "tensor"),
    )
    out_specs = (
        P("fsdp", None, None, None),
        P("fsdp", None, None, None),
        P("fsdp", None, "tensor"),
        P("fsdp", None, "tensor"),
        P("fsdp", None, "tensor"),
        P("tensor", "fsdp"),
        P("tensor", "fsdp"),
        P("tensor", "fsdp"),
        P("fsdp", "tensor"),
        P("fsdp", "tensor"),
        P("fsdp", "tensor"),
        P("tensor", "fsdp"),
        P("tensor", "fsdp"),
        P("tensor", "fsdp"),
        P(),
        P(),
        P(),
        P(None, "tensor"),
        P(None, "tensor"),
        P(None, "tensor"),
        P("tensor"),
        P("tensor"),
        P("tensor"),
        P(None, "tensor"),
        P(None, "tensor"),
        P(None, "tensor"),
    )
    return jax.shard_map(
        on_device, mesh=mesh, in_specs=in_specs, out_specs=out_specs, check_vma=False
    )
```

```python
import types

import jax
import jax.numpy as jnp
from jax import lax
from jax.experimental import pallas as pl
from jax.experimental.pallas import tpu as pltpu
from jax.sharding import PartitionSpec as P

MESH = pl.DeviceIdType.MESH
LOW = jnp.bfloat16
FULL = jnp.float32
EPS = 1e-5
SCALE = 32.0 ** -0.5
BLOCKED = -1e30
STEP = 10
REL = 169
BETA_ONE = 0.9
BETA_TWO = 0.999
ADAM_EPS = 1e-08
RATE_MATRIX = 0.1
RATE_VECTOR = 0.2
RATE_TABLE = 0.5
WEIGHT_DECAY = 0.05
ORDERS = ((0, 1, 2), (1, 2, 0), (2, 0, 1))
SUMS = (((0, 1, 2), (1, 0, 2), (1, 0, 2)), ((0, 1, 2), (1, 0, 2), (0, 1, 2)))
WIDTHS = (128, 384)


class Place:
    def __init__(self):
        f = lax.axis_index("fsdp")
        self.t = lax.axis_index("tensor")
        x, y = f % 4, f // 8
        z = ((f // 4) % 2) * 2 + self.t // 2
        self.core = self.t % 2
        self.at = (x, y, z)
        mate = (x, y, (z // 2) * 2 + 1 - z % 2)
        self.sibling = self.device(core=1 - self.core)
        self.z_mate = self.device(mate)
        self.across = self.device(mate, 1 - self.core)
        self.mate_t = (1 - z % 2) * 2 + self.core

    def device(self, at=None, core=None):
        x, y, z = self.at if at is None else at
        core = self.core if core is None else core
        return (y * 8 + (z // 2) * 4 + x, (z % 2) * 2 + core)

    def along(self, axis, by):
        at = list(self.at)
        at[axis] = (at[axis] + by + 4) % 4
        return self.device(at)


def block_of(ref, lead, place, core, full, axis=None, shift=0, half=None):
    whole = slice(None)
    at = list(place.at)
    if axis is not None:
        at[axis] = (at[axis] + shift + 4) % 4
    x, y, z = at
    x = whole if 0 in full else x
    y = whole if 1 in full else y
    low, high = (whole, whole) if 2 in full else (z % 2, z // 2)
    low = low if half is None else half
    return ref.at[(*lead, low, core, y, high, x)] if core is not None else ref.at[(*lead, low, y, high, x)]


def block_dims(full):
    return tuple(size for axis, size in ((2, 2), (1, 4), (2, 2), (0, 4)) if axis in full)


def each(dims, fn):
    outer = dims[:-1]
    count = 1
    for size in outer:
        count *= size
    if count == 1:
        fn((0,) * len(outer))
        return

    def body(n, _):
        index = []
        for size in reversed(outer):
            index.append(n % size)
            n = n // size
        fn(tuple(reversed(index)))
        return 0

    lax.fori_loop(0, count, body, 0)


def mm(a, b):
    return lax.dot_general(a, b, (((1,), (0,)), ((), ())), preferred_element_type=FULL)


def mm_nt(a, b):
    return lax.dot_general(a, b, (((1,), (1,)), ((), ())), preferred_element_type=FULL)


def mm_tn(a, b):
    return lax.dot_general(a, b, (((0,), (0,)), ((), ())), preferred_element_type=FULL)


def three_lows(a):
    high = a.astype(LOW)
    rest = a - high.astype(FULL)
    middle = rest.astype(LOW)
    last = (rest - middle.astype(FULL)).astype(LOW)
    return jnp.concatenate([high, middle, last], axis=0)


def normed(v):
    center = v - jnp.mean(v, axis=-1, keepdims=True)
    r = lax.rsqrt(jnp.mean(center * center, axis=-1, keepdims=True) + EPS)
    return center * r, r


def norm_back(n, x, r, offset):
    q = n * (1.0 + offset)
    return r * (q - jnp.mean(q, axis=-1, keepdims=True) - x * jnp.mean(q * x, axis=-1, keepdims=True))


def gelu_parts(u):
    size = jnp.abs(u)
    k = 1.0 / (1.0 + (0.3275911 * 0.7071067811865476) * size)
    bell = jnp.exp(-0.5 * u * u)
    poly = k * (0.254829592 + k * (-0.284496736 + k * (1.421413741 + k * (-1.453152027 + k * 1.061405429))))
    tail = 0.5 * poly * bell
    share = jnp.where(u < 0, tail, 1.0 - tail)
    return u * share, share + u * bell * 0.3989422804014327


def lane_mask(h):
    lane = lax.broadcasted_iota(jnp.int32, (128, 128), 1)
    return (lane >= h * 32) & (lane < h * 32 + 32)


def keep(mask, a):
    return jnp.where(mask, a, jnp.zeros_like(a))


def spans():
    for image in range(2):
        for r in range(14):
            for side in range(2):
                window = image * 4 + (r // 7) * 2 + side
                yield image, r * 14 + side * 7, window * 64 + (r % 7) * 7


def block_kernel(ref):
    images, cotangents, vec, idx = ref.images, ref.cotangents, ref.vec, ref.idx
    w = (ref.w1, ref.w2)
    g = (ref.g1, ref.g2)
    sib = (ref.sib1, ref.sib2)
    gs, small, steps = ref.gs, ref.small, ref.steps
    tok, cot, cot_low, cot_t = ref.tok, ref.cot, ref.cot_low, ref.cot_t
    n1, n1_t, x1, r1 = ref.n1, ref.n1_t, ref.x1, ref.r1
    n2, n2_t, x2, r2 = ref.n2, ref.n2_t, ref.x2, ref.r2
    qkv, probs, att, mid, hid, gpre = ref.qkv, ref.probs, ref.att, ref.mid, ref.hid, ref.gpre
    gmid, gml, gml_t, dqkv = ref.gmid, ref.gml, ref.gml_t, ref.dqkv
    onehot, spread, bias, dsum, table = ref.onehot, ref.spread, ref.bias, ref.dsum, ref.table
    stage, field, outs = ref.stage, ref.field, ref.outs
    local = ref.local_sem

    place = Place()
    t_own, core = place.t, place.core
    barrier = pltpu.get_barrier_semaphore()
    partners = [place.along(axis, by) for axis in range(3) for by in (1, 2, 3)] + [place.sibling, place.across]
    for device in partners:
        pl.semaphore_signal(barrier, inc=1, device_id=device, device_id_type=MESH)

    copies_in = [
        pltpu.make_async_copy(images, ref.img, local.at[0]),
        pltpu.make_async_copy(cotangents, ref.cimg, local.at[1]),
    ]
    for copy in copies_in:
        copy.start()

    sends = []

    def send(src, dst, out, into, device):
        copy = pltpu.make_async_remote_copy(src, dst, out, into, device, MESH)
        copy.start()
        sends.append(copy)

    def wait_in(block, out, into):
        pltpu.make_async_remote_copy(block, block, out, into, place.sibling, MESH).wait_recv()

    x, y, z = place.at
    own = (z % 2, core, y, z // 2, x)
    for p in range(3):
        w[0][(p, *own)] = ref.attn[p].astype(LOW)
    proj, up, down = ref.proj[...].astype(LOW), ref.up[...].astype(LOW), ref.down[...].astype(LOW)
    w[1][(0, *own)] = jnp.concatenate([proj, up[:, 0:256]], axis=1)
    w[1][(1, *own)] = jnp.concatenate([up[:, 256:512], down[:, 0:128]], axis=1)
    w[1][(2, *own)] = down[:, 128:512]
    mine = gs.at[t_own]
    mine[...] = jnp.zeros((16, 128), FULL)
    mine[0:4, :] = ref.rel[:, 0:128]
    mine[4:8, 0 : REL - 128] = ref.rel[:, 128:REL]
    mine[8:10, :] = ref.head[...]
    for k in range(4):
        mine[10 + k : 11 + k, :] = ref.unit[:, k * 128 : (k + 1) * 128]

    pl.semaphore_wait(barrier, len(partners))

    in_sem, out_sem, sib_in, sib_out = ref.w_in, ref.w_out, ref.ws_in, ref.ws_out

    def gather_start(b, phase):
        for p in range(3):
            axis, done = ORDERS[p][phase], ORDERS[p][:phase]
            block = block_of(w[b], (p,), place, core, done)
            for shift in (1, 3, 2):
                at = (b, p, phase, shift - 1)
                send(block, block, out_sem.at[at], in_sem.at[at], place.along(axis, shift))
            if phase == 2:
                send(block, block, sib_out.at[b, p, 0], sib_in.at[b, p, 0], place.sibling)

    def gather_finish(b, phase, shifts=(1, 3, 2)):
        for shift in shifts:
            for p in range(3):
                axis, done = ORDERS[p][phase], ORDERS[p][:phase]
                block = block_of(w[b], (p,), place, core, done, axis, -shift)
                at = (b, p, phase, shift - 1)
                wait_in(block, out_sem.at[at], in_sem.at[at])
                if phase == 2:
                    send(block, block, sib_out.at[b, p, shift], sib_in.at[b, p, shift], place.sibling)

    def gather_last(b):
        for p in range(3):
            axis, done = ORDERS[p][2], ORDERS[p][:2]
            for shift in range(4):
                block = block_of(w[b], (p,), place, 1 - core, done, axis, -shift)
                wait_in(block, sib_out.at[b, p, shift], sib_in.at[b, p, shift])

    mates = (place.sibling, place.z_mate, place.across)
    mate_ts = (t_own + 1 - 2 * core, place.mate_t, (1 - z % 2) * 2 + 1 - core)
    gather_start(0, 0)
    gather_start(1, 0)
    for k in range(3):
        send(mine, mine, ref.s_out.at[k], ref.s_in.at[k], mates[k])

    wide = ref.wide
    wide[...] = jnp.full((56, 128), -1, jnp.int32)
    wide[0:49, 0:49] = idx[...]
    wide[0:49, 64:113] = idx[...]
    row_id = lax.broadcasted_iota(jnp.int32, (256, 128), 0)
    for i in range(49):
        onehot[:, i * 128 : (i + 1) * 128] = (row_id == wide[i : i + 1, :]).astype(FULL).astype(LOW)
    small[...] = jnp.zeros((16, 768), FULL)
    tok[...] = jnp.zeros((512, 512), FULL)
    cot[...] = jnp.zeros((512, 512), FULL)
    gather_finish(0, 0)
    gather_start(0, 1)
    gather_finish(1, 0)
    gather_start(1, 1)
    for n, (source, copy, dst) in enumerate(zip((ref.img, ref.cimg), copies_in, (tok, cot))):
        copy.wait()
        if n == 1:
            gather_finish(0, 1)
            gather_start(0, 2)
            gather_finish(1, 1)

        def widen(k, _):
            rows = pl.ds(pl.multiple_of(k * 112, 112), 112)
            for k4 in range(4):
                stage[k4, rows, :] = source[rows, k4 * 128 : (k4 + 1) * 128].astype(FULL)
            return 0

        lax.fori_loop(0, 14, widen, 0)
        for image, first, top in spans():
            for k in range(4):
                dst[top : top + 7, k * 128 : (k + 1) * 128] = stage[
                    k, pl.ds(first * 8 + image + 2 * t_own, 7, stride=8), :
                ]
    gather_finish(0, 2, (1, 3))
    gather_start(1, 2)

    def start(k, _):
        rows = pl.ds(pl.multiple_of(k * 64, 64), 64)
        xs, r = normed(tok[rows, :])
        x1[rows, :] = xs
        r1[rows, :] = r
        n1[rows, :] = (xs * (1.0 + vec[0:1, :]) + vec[1:2, :]).astype(LOW)
        c = cot[rows, :]
        cot_low[rows, :] = c.astype(LOW)
        small[5:6, 0:512] += jnp.sum(c, axis=0, keepdims=True)
        return 0

    lax.fori_loop(0, 8, start, 0)
    n1_t[...] = n1[...].T
    cot_t[...] = cot_low[...].T
    gather_finish(0, 2, (2,))
    for k in range(3):
        wait_in(gs.at[mate_ts[k]], ref.s_out.at[k], ref.s_in.at[k])
    for t in range(4):
        table[t * 4 : t * 4 + 4, 0:128] = gs[t, 0:4, :]
        table[t * 4 : t * 4 + 4, 128:256] = gs[t, 4:8, :]
    spread[...] = mm(three_lows(table[...]), onehot[...])
    lane = lax.broadcasted_iota(jnp.int32, (16, 128), 1)
    low_side = lane < 49
    high_side = (lane >= 64) & (lane < 113)
    for i in range(64):
        if i < 49:
            at = slice(i * 128, (i + 1) * 128)
            line = spread[0:16, at] + spread[16:32, at] + spread[32:48, at]
        else:
            line = jnp.zeros((16, 128), FULL)
        bias[i * 16 : (i + 1) * 16, :] = jnp.where(low_side, line, BLOCKED)
        bias[(64 + i) * 16 : (65 + i) * 16, :] = jnp.where(high_side, line, BLOCKED)
    gather_last(0)

    def columns(b, p, t, a, z):
        return w[b][p, t // 2, t % 2, :, :, :, :, a:z].reshape(512, z - a)

    def w_qkv(t):
        return jnp.concatenate([columns(0, c, t, 0, 128) for c in range(3)], axis=1)

    def w_proj(t):
        return columns(1, 0, t, 0, 128)

    def w_up(t):
        return jnp.concatenate([columns(1, 0, t, 128, 384), columns(1, 1, t, 0, 256)], axis=1)

    def w_down(t):
        return jnp.concatenate([columns(1, 1, t, 256, 384), columns(1, 2, t, 0, 384)], axis=1)

    def put_grad(b, p, t, a, value):
        g[b][p, t // 2, t % 2, :, :, :, :, a : a + value.shape[1]] = value.astype(LOW).reshape(
            4, 2, 4, 16, value.shape[1]
        )

    near = ref.near

    def by_head(a):
        return jnp.concatenate([keep(lane_mask(h), a) for h in range(4)], axis=0)

    def heads_wide(a):
        return jnp.concatenate([a[h * 128 : (h + 1) * 128] for h in range(4)], axis=1)

    def forward(t, _):
        mixed = mm(n1[...], w_qkv(t))
        q_bias, v_bias = gs[t, 8:9, :], gs[t, 9:10, :]
        qkv[t, 0] = (mixed[:, 0:128] + q_bias).astype(LOW)
        qkv[t, 1] = mixed[:, 128:256].astype(LOW)
        qkv[t, 2] = (mixed[:, 256:384] + v_bias).astype(LOW)
        for h in range(4):
            near[h * 128 : (h + 1) * 128, :] = bias[pl.ds(t * 4 + h, 128, stride=16), :]
        for wp in range(4):
            rows = slice(wp * 128, (wp + 1) * 128)
            q, k, v = qkv[t, 0, rows], qkv[t, 1, rows], qkv[t, 2, rows]
            s = mm_nt(by_head(q), k) * SCALE + near[...]
            e = jnp.exp(s - jnp.max(s, axis=-1, keepdims=True))
            p = (e * (1.0 / jnp.sum(e, axis=-1, keepdims=True))).astype(LOW)
            probs[t, wp] = p
            att[t, rows] = mm(heads_wide(p), by_head(v)).astype(LOW)
        return 0

    lax.fori_loop(0, 3, forward, 0)
    gather_finish(1, 2, (1, 3))
    lax.fori_loop(3, 4, forward, 0)
    gather_finish(1, 2, (2,))
    gather_last(1)

    def second(k, _):
        rows = pl.ds(pl.multiple_of(k * 128, 128), 128)
        acc = tok[rows, :] + (mid[rows, :] + vec[2:3, :])
        mid[rows, :] = acc
        xs, r = normed(acc)
        x2[rows, :] = xs
        r2[rows, :] = r
        n2[rows, :] = (xs * (1.0 + vec[3:4, :]) + vec[4:5, :]).astype(LOW)
        return 0

    mid[...] = mm_nt(
        jnp.concatenate([att[t] for t in range(4)], axis=1), jnp.concatenate([w_proj(t) for t in range(4)], axis=1)
    )
    lax.fori_loop(0, 4, second, 0)
    gmid[...] = jnp.zeros((512, 512), FULL)
    n2_t[...] = n2[...].T

    ghid = ref.ghid

    def feed(t, _):
        unit = jnp.concatenate([gs[t, 10 + k : 11 + k, :] for k in range(4)], axis=1)
        up_t, down_t = w_up(t), w_down(t)

        tok[...] = mm(n2[...], up_t) + unit
        ghid[...] = mm(cot_low[...], down_t)

        def rows_of(k, total):
            rows = pl.ds(pl.multiple_of(k * 64, 64), 64)
            value, slope = gelu_parts(tok[rows, :])
            hid[t, rows, :] = value.astype(LOW)
            grad = ghid[rows, :] * slope
            gpre[t, rows, :] = grad.astype(LOW)
            return total + jnp.sum(grad, axis=0, keepdims=True)

        small[pl.ds(8 + t, 1), 0:512] = lax.fori_loop(0, 8, rows_of, jnp.zeros((1, 512), FULL))
        grad_up = mm(n2_t[...], gpre[t])
        put_grad(1, 0, t, 128, grad_up[:, 0:256])
        put_grad(1, 1, t, 0, grad_up[:, 256:512])
        grad_down = mm(cot_t[...], hid[t])
        put_grad(1, 1, t, 256, grad_down[:, 0:128])
        put_grad(1, 2, t, 0, grad_down[:, 128:512])
        mid[...] += mm_nt(hid[t], down_t)
        gmid[...] += mm_nt(gpre[t], up_t)
        return 0

    g_in, g_out, gs_in, gs_out = ref.g_in, ref.g_out, ref.gs_in, ref.gs_out
    slot = ref.slots

    def sum_core(b, p, half):
        axis, full = SUMS[b][p][0], SUMS[b][p][1:]
        for shift in (1, 3, 2, 0):
            src = block_of(g[b], (p,), place, 1 - core, full, axis, shift, half)
            dst = block_of(sib[b], (p,), place, None, full, axis, shift, half)
            send(src, dst, gs_out.at[b, p, shift, half], gs_in.at[b, p, shift, half], place.sibling)

    def sum_first(b, p, half):
        axis, full = SUMS[b][p][0], SUMS[b][p][1:]
        for shift in (1, 3, 2, 0):
            here = block_of(g[b], (p,), place, core, full, axis, shift, half)
            there = block_of(sib[b], (p,), place, None, full, axis, shift, half)
            wait_in(there, gs_out.at[b, p, shift, half], gs_in.at[b, p, shift, half])

            def add(index):
                here[index] = here[index] + there[index]

            each(block_dims(full)[1:], add)
            if shift:
                at = (b, p, 0, shift - 1, half)
                send(here, slot[b, p, 0].at[shift - 1, half], g_out.at[at], g_in.at[at], place.along(axis, shift))

    def sum_start(b, p, phase):
        axis, full = SUMS[b][p][phase], SUMS[b][p][phase + 1 :]
        for shift in (1, 3, 2):
            here = block_of(g[b], (p,), place, core, full, axis, shift)
            at = (b, p, phase, shift - 1, 0)
            send(here, slot[b, p, phase].at[shift - 1], g_out.at[at], g_in.at[at], place.along(axis, shift))

    def sum_finish(b, p, phase):
        axis, full = SUMS[b][p][phase], SUMS[b][p][phase + 1 :]
        here = block_of(g[b], (p,), place, core, full)
        came = [slot[b, p, phase].at[k] for k in range(3)]
        for k in range(3):
            for half in range(2 if phase == 0 else 1):
                at = (b, p, phase, k, half)
                wait_in(came[k].at[half] if phase == 0 else came[k], g_out.at[at], g_in.at[at])

        def total(index):
            one, two, three = (c[index].astype(FULL) for c in came)
            return (here[index].astype(FULL) + one) + (two + three)

        if phase == 2:
            return total(())

        def add(index):
            here[index] = total(index).astype(LOW)

        each(block_dims(full), add)
        return None

    lax.fori_loop(0, 2, feed, 0)
    for p in (1, 2):
        sum_core(1, p, 0)
    lax.fori_loop(2, 3, feed, 0)
    for p in (1, 2):
        sum_first(1, p, 0)
    lax.fori_loop(3, 4, feed, 0)
    for p in (1, 2):
        sum_core(1, p, 1)

    def third(k, _):
        rows = pl.ds(pl.multiple_of(k * 128, 128), 128)
        mid[rows, :] += vec[5:6, :]
        n = gmid[rows, :]
        xs = x2[rows, :]
        grad = cot[rows, :] + norm_back(n, xs, r2[rows, :], vec[3:4, :])
        gmid[rows, :] = grad
        gml[rows, :] = grad.astype(LOW)
        small[2:3, 0:512] += jnp.sum(grad, axis=0, keepdims=True)
        small[3:4, 0:512] += jnp.sum(n * xs, axis=0, keepdims=True)
        small[4:5, 0:512] += jnp.sum(n, axis=0, keepdims=True)
        return 0

    lax.fori_loop(0, 4, third, 0)
    for p in (1, 2):
        sum_first(1, p, 1)
    gml_t[...] = gml[...].T

    def proj_grad(t, _):
        put_grad(1, 0, t, 0, mm(gml_t[...], att[t]))
        return 0

    lax.fori_loop(0, 4, proj_grad, 0)
    for half in range(2):
        sum_core(1, 0, half)

    o_in, o_out = ref.o_in, ref.o_out

    def give(n, half, src):
        rows = pl.ds(half * 208, 208)
        for image, first, top in spans():
            if image == half:
                field[half * 208 + first : half * 208 + first + 7, :] = src[top : top + 7, :]
        outs[n, t_own, rows, :] = field[rows, :].astype(LOW)
        block = outs.at[n, t_own, rows]
        send(block, block, o_out.at[n, half, 1], o_in.at[n, half, 1], place.z_mate)
        send(block, block, o_out.at[n, half, 0], o_in.at[n, half, 0], place.sibling)

    def came(n, half, kind):
        t = mate_ts[kind]
        block = outs.at[n, t, pl.ds(half * 208, 208)]
        wait_in(block, o_out.at[n, half, kind], o_in.at[n, half, kind])
        if kind == 1:
            send(block, block, o_out.at[n, half, 2], o_in.at[n, half, 2], place.sibling)

    def take(n, half, t):
        field[0:208, :] = outs[n, t, half * 208 : half * 208 + 208, :].astype(FULL)
        for k in range(4):
            stage[k, pl.ds(2 * t + half, 196, stride=8), :] = field[0:196, k * 128 : (k + 1) * 128]

    def take_near(n):
        for half in range(2):
            take(n, half, t_own)
            came(n, half, 0)
            take(n, half, mate_ts[0])

    def take_far(n):
        for half in range(2):
            take(n, half, mate_ts[1])
        for half in range(2):
            came(n, half, 2)
            take(n, half, mate_ts[2])

    field[...] = jnp.zeros((416, 512), FULL)
    give(0, 0, mid)
    give(0, 1, mid)
    for half in range(2):
        sum_first(1, 0, half)

    def backward(image, t):
        span = slice(image * 256, image * 256 + 256)
        ga = mm(gml[span, :], w_proj(t)).astype(LOW)
        sums = jnp.zeros((512, 128), FULL)
        sum_q = jnp.zeros((1, 128), FULL)
        sum_v = jnp.zeros((1, 128), FULL)
        for n in range(2):
            wp = image * 2 + n
            rows = slice(wp * 128, (wp + 1) * 128)
            q, k, v = qkv[t, 0, rows], qkv[t, 1, rows], qkv[t, 2, rows]
            grad = by_head(ga[n * 128 : (n + 1) * 128])
            p_low = probs[t, wp]
            p = p_low.astype(FULL)
            dp = mm_nt(grad, v)
            ds = (p * (dp - jnp.sum(dp * p, axis=-1, keepdims=True))).astype(LOW)
            sums = sums + ds.astype(FULL)
            dq = (mm(heads_wide(ds), by_head(k)) * SCALE).astype(LOW)
            dk = (mm_tn(ds, by_head(q)) * SCALE).astype(LOW)
            dv = mm_tn(p_low, grad).astype(LOW)
            dqkv[t, rows, 0:128] = dq
            dqkv[t, rows, 128:256] = dk
            dqkv[t, rows, 256:384] = dv
            sum_q = sum_q + jnp.sum(dq.astype(FULL), axis=0, keepdims=True)
            sum_v = sum_v + jnp.sum(dv.astype(FULL), axis=0, keepdims=True)
        for h in range(4):
            at = pl.ds(t * 4 + h, 128, stride=16)
            value = sums[h * 128 : (h + 1) * 128]
            dsum[at, :] = value + dsum[at, :] if image else value
        at = pl.ds(pl.multiple_of(t * 128, 128), 128)
        small[6:7, at] += sum_q
        small[7:8, at] += sum_v
        tok[span, :] += mm_nt(dqkv[t, span, :], w_qkv(t))
        if image:
            grad = mm(n1_t[...], dqkv[t])
            for c in range(3):
                put_grad(0, c, t, 0, grad[:, c * 128 : (c + 1) * 128])

    def backward_first(t, _):
        backward(0, t)
        return 0

    def backward_second(t, _):
        backward(1, t)
        return 0

    def last(k, _):
        rows = pl.ds(pl.multiple_of(k * 128, 128), 128)
        n = tok[rows, :]
        xs = x1[rows, :]
        gmid[rows, :] += norm_back(n, xs, r1[rows, :], vec[0:1, :])
        small[0:1, 0:512] += jnp.sum(n * xs, axis=0, keepdims=True)
        small[1:2, 0:512] += jnp.sum(n, axis=0, keepdims=True)
        return 0

    tok[...] = jnp.zeros((512, 512), FULL)
    lax.fori_loop(0, 4, backward_first, 0)
    lax.fori_loop(0, 2, last, 0)
    give(1, 0, gmid)
    lax.fori_loop(0, 2, backward_second, 0)
    for p in range(3):
        sum_core(0, p, 0)
    lax.fori_loop(2, 3, backward_second, 0)
    for p in range(3):
        sum_first(0, p, 0)
    lax.fori_loop(3, 4, backward_second, 0)
    for p in range(3):
        sum_core(0, p, 1)
    lax.fori_loop(2, 4, last, 0)
    give(1, 1, gmid)
    for p in range(3):
        sum_first(0, p, 1)
    lines = []
    for i in range(49):
        lines.append(three_lows(dsum[i * 16 : (i + 1) * 16, :] + dsum[(64 + i) * 16 : (65 + i) * 16, :]))
    table_sum = mm_nt(jnp.concatenate(lines, axis=1), onehot[...])
    small[:, 512:768] = table_sum[0:16] + table_sum[16:32] + table_sum[32:48]

    n_in, n_out = ref.n_in, ref.n_out

    def small_start(k):
        if k < 3:
            block = steps.at[k, place.at[k]]
            for shift in (1, 3, 2):
                send(block, block, n_out.at[k, shift - 1], n_in.at[k, shift - 1], place.along(k, shift))
        else:
            block = steps.at[3, core]
            send(block, block, n_out.at[3, 0], n_in.at[3, 0], place.sibling)

    def small_finish(k):
        if k < 3:
            for shift in (1, 3, 2):
                at = (place.at[k] - shift + 4) % 4
                wait_in(steps.at[k, at], n_out.at[k, shift - 1], n_in.at[k, shift - 1])
            return (steps[k, 0] + steps[k, 1]) + (steps[k, 2] + steps[k, 3])
        wait_in(steps.at[3, 1 - core], n_out.at[3, 0], n_in.at[3, 0])
        return steps[3, 0] + steps[3, 1]

    def small_next(k):
        value = small_finish(k)
        steps[k + 1, place.at[k + 1] if k < 2 else core] = value
        small_start(k + 1)

    steps[0, place.at[0]] = small[...]
    small_start(0)
    for half in range(2):
        came(0, half, 1)
    came(1, 0, 1)
    take_near(0)
    for p in range(3):
        sum_finish(0, p, 0)
        sum_start(0, p, 1)
    small_next(0)
    for p in range(3):
        sum_finish(1, p, 0)
        sum_start(1, p, 1)
    take_far(0)

    def narrow(k, _):
        rows = pl.ds(pl.multiple_of(k * 112, 112), 112)
        for k4 in range(4):
            ref.block_out[rows, k4 * 128 : (k4 + 1) * 128] = stage[k4, rows, :].astype(LOW)
        return 0

    lax.fori_loop(0, 14, narrow, 0)
    for p in range(3):
        sum_finish(0, p, 1)
        sum_start(0, p, 2)
    small_next(1)
    for p in range(3):
        sum_finish(1, p, 1)
        sum_start(1, p, 2)
    take_near(1)
    came(1, 1, 1)
    for p in range(3):
        ref.attn_grad[p] = sum_finish(0, p, 2)
    small_next(2)
    first, second_, third_ = (sum_finish(1, p, 2) for p in range(3))
    ref.proj_grad[...] = first[:, 0:128]
    ref.up_grad[:, 0:256] = first[:, 128:384]
    ref.up_grad[:, 256:512] = second_[:, 0:256]
    ref.down_grad[:, 0:128] = second_[:, 256:384]
    ref.down_grad[:, 128:512] = third_
    take_far(1)
    ref.total[...] = small_finish(3)
    results = []
    for k in range(4):
        lanes = ref.images_grad.at[:, pl.ds(k * 128, 128)]
        results.append(pltpu.make_async_copy(stage.at[k], lanes, local.at[k]))
        results[k].start()
    for copy in sends:
        copy.wait_send()
    for copy in results:
        copy.wait()


def run_block(images, cotangents, vec, idx, attn, proj, up, down, rel, head, unit):
    whole = pl.BlockSpec(memory_space=pltpu.VMEM)
    anywhere = pl.BlockSpec(memory_space=pl.ANY)
    ins = dict(
        images=anywhere, cotangents=anywhere, vec=whole, idx=whole, attn=whole, proj=whole,
        up=whole, down=whole, rel=whole, head=whole, unit=whole,
    )
    results = dict(
        block_out=((1568, 512), LOW, whole),
        images_grad=((1568, 512), FULL, anywhere),
        attn_grad=((3, 16, 128), FULL, whole),
        proj_grad=((16, 128), FULL, whole),
        up_grad=((16, 512), FULL, whole),
        down_grad=((16, 512), FULL, whole),
        total=((16, 768), FULL, whole),
    )
    square = (512, 512)
    scratch = dict(
        img=pltpu.VMEM((1568, 512), LOW),
        cimg=pltpu.VMEM((1568, 512), LOW),
        w1=pltpu.VMEM((3, 2, 2, 4, 2, 4, 16, 128), LOW),
        w2=pltpu.VMEM((3, 2, 2, 4, 2, 4, 16, 384), LOW),
        g1=pltpu.VMEM((3, 2, 2, 4, 2, 4, 16, 128), LOW),
        g2=pltpu.VMEM((3, 2, 2, 4, 2, 4, 16, 384), LOW),
        sib1=pltpu.VMEM((3, 2, 4, 2, 4, 16, 128), LOW),
        sib2=pltpu.VMEM((3, 2, 4, 2, 4, 16, 384), LOW),
        gs=pltpu.VMEM((4, 16, 128), FULL),
        small=pltpu.VMEM((16, 768), FULL),
        steps=pltpu.VMEM((4, 4, 16, 768), FULL),
        qkv=pltpu.VMEM((4, 3, 512, 128), LOW),
        probs=pltpu.VMEM((4, 4, 512, 128), LOW),
        att=pltpu.VMEM((4, 512, 128), LOW),
        hid=pltpu.VMEM((4, 512, 512), LOW),
        gpre=pltpu.VMEM((4, 512, 512), LOW),
        dqkv=pltpu.VMEM((4, 512, 384), LOW),
        onehot=pltpu.VMEM((256, 49 * 128), LOW),
        spread=pltpu.VMEM((48, 49 * 128), FULL),
        bias=pltpu.VMEM((2048, 128), FULL),
        dsum=pltpu.VMEM((2048, 128), FULL),
        table=pltpu.VMEM((16, 256), FULL),
        wide=pltpu.VMEM((56, 128), jnp.int32),
        near=pltpu.VMEM((512, 128), FULL),
        stage=pltpu.VMEM((4, 1568, 128), FULL),
        field=pltpu.VMEM((416, 512), FULL),
        outs=pltpu.VMEM((2, 4, 416, 512), LOW),
        r1=pltpu.VMEM((512, 1), FULL),
        r2=pltpu.VMEM((512, 1), FULL),
    )
    full, low = pltpu.VMEM(square, FULL), pltpu.VMEM(square, LOW)
    scratch.update(ghid=full, tok=full, cot=full, x1=full, x2=full, mid=full, gmid=full)
    scratch.update(cot_low=low, cot_t=low, n1=low, n1_t=low, n2=low, n2_t=low, gml=low, gml_t=low)
    slots = {}
    for b in range(2):
        for p in range(3):
            for phase in range(3):
                slots[b, p, phase] = pltpu.VMEM((3, *block_dims(SUMS[b][p][phase + 1 :]), 16, WIDTHS[b]), LOW)
    sems = dict(
        local_sem=(4,), w_in=(2, 3, 3, 3), w_out=(2, 3, 3, 3), ws_in=(2, 3, 4), ws_out=(2, 3, 4),
        s_in=(3,), s_out=(3,), g_in=(2, 3, 3, 3, 2), g_out=(2, 3, 3, 3, 2), gs_in=(2, 3, 4, 2), gs_out=(2, 3, 4, 2),
        o_in=(2, 2, 3), o_out=(2, 2, 3), n_in=(4, 3), n_out=(4, 3),
    )
    for name, shape in sems.items():
        scratch[name] = pltpu.SemaphoreType.DMA(shape)
    names = [*ins, *results, *scratch]

    def kernel(*refs):
        named = dict(zip(names, refs))
        block_kernel(types.SimpleNamespace(**named, slots=dict(zip(slots, refs[len(names) :]))))

    return pl.pallas_call(
        kernel,
        out_shape=tuple(jax.ShapeDtypeStruct(shape, dtype) for shape, dtype, _ in results.values()),
        in_specs=list(ins.values()),
        out_specs=[spec for _, _, spec in results.values()],
        scratch_shapes=[*scratch.values(), *slots.values()],
        compiler_params=pltpu.CompilerParams(
            collective_id=0, has_side_effects=True, vmem_limit_bytes=63 * 2**20
        ),
        name="block_forward_backward",
    )(images, cotangents, vec, idx, attn, proj, up, down, rel, head, unit)


def adam_step(weight, grad, first, second, rate, decay):
    first_new = BETA_ONE * first + (1.0 - BETA_ONE) * grad
    second_new = BETA_TWO * second + (1.0 - BETA_TWO) * grad * grad
    first_hat = first_new / (1.0 - BETA_ONE**STEP)
    second_hat = second_new / (1.0 - BETA_TWO**STEP)
    updated = weight - rate * (first_hat / (jnp.sqrt(second_hat) + ADAM_EPS) + decay * weight)
    return (updated, first_new, second_new)


PARAMETERS = (
    ((3, 16, 128), RATE_MATRIX, WEIGHT_DECAY),
    ((16, 128), RATE_MATRIX, WEIGHT_DECAY),
    ((16, 512), RATE_MATRIX, WEIGHT_DECAY),
    ((16, 512), RATE_MATRIX, WEIGHT_DECAY),
    ((6, 512), RATE_VECTOR, 0.0),
    ((2, 128), RATE_VECTOR, 0.0),
    ((1, 512), RATE_VECTOR, 0.0),
    ((4, REL), RATE_TABLE, 0.0),
)


def update_kernel(*refs):
    refs = list(refs)

    def some(count):
        taken = refs[:count]
        del refs[:count]
        return taken

    results, grads, states = some(2), some(5), some(24)
    results_out, states_out = some(2), some(24)
    held, grads_in, states_in, states_new = some(2), some(5), some(24), some(24)
    sems_in, sems_out = refs
    arriving = []
    leaving = []
    for n, (source, page, target) in enumerate(zip(results, held, results_out)):
        for k in range(2):
            rows = pl.ds(k * 784, 784)
            at = 2 * n + k
            arriving.append(pltpu.make_async_copy(source.at[rows], page.at[rows], sems_in.at[29 + at]))
            leaving.append(pltpu.make_async_copy(page.at[rows], target.at[rows], sems_out.at[24 + at]))
    loads = [
        pltpu.make_async_copy(a, b, sems_in.at[n]) for n, (a, b) in enumerate(zip(grads + states, grads_in + states_in))
    ]
    for copy in loads + arriving:
        copy.start()
    for copy in loads:
        copy.wait()
    t = lax.axis_index("tensor")
    total = grads_in[4]

    def picked(pieces):
        value = pieces[3]
        for k in (2, 1, 0):
            value = jnp.where(t == k, pieces[k], value)
        return value

    small = (
        total[0:6, 0:512],
        picked([total[6:8, k * 128 : (k + 1) * 128] for k in range(4)]),
        picked([total[8 + k : 9 + k, 0:512] for k in range(4)]),
        picked([total[4 * k : 4 * k + 4, 512 : 512 + REL] for k in range(4)]),
    )
    for coming, going in zip(arriving, leaving):
        coming.wait()
        going.start()
    stores = []
    for n, (_, rate, decay) in enumerate(PARAMETERS):
        grad = grads_in[n][...] if n < 4 else small[n - 4]
        weight, first, second = (states_in[3 * n + k][...] for k in range(3))
        for k, value in enumerate(adam_step(weight, grad, first, second, rate, decay)):
            at = 3 * n + k
            states_new[at][...] = value
            copy = pltpu.make_async_copy(states_new[at], states_out[at], sems_out.at[at])
            copy.start()
            stores.append(copy)
    for copy in stores + leaving:
        copy.wait()


def update(results, grads, states):
    anywhere = pl.BlockSpec(memory_space=pl.ANY)
    shapes = [shape for shape, _, _ in PARAMETERS for _ in range(3)]
    inner = [pltpu.VMEM(shape, FULL) for shape in shapes]
    out_shape = [jax.ShapeDtypeStruct(a.shape, a.dtype) for a in results]
    out_shape += [jax.ShapeDtypeStruct(shape, FULL) for shape in shapes]
    return pl.pallas_call(
        update_kernel,
        out_shape=out_shape,
        in_specs=[anywhere] * 31,
        out_specs=[anywhere] * 26,
        scratch_shapes=[
            *[pltpu.VMEM(a.shape, a.dtype) for a in [*results, *grads]], *inner, *inner,
            pltpu.SemaphoreType.DMA((33,)), pltpu.SemaphoreType.DMA((28,)),
        ],
        compiler_params=pltpu.CompilerParams(vmem_limit_bytes=60 * 2**20),
        name="adam_update",
    )(*results, *grads, *states)


def on_device(
    images,
    out_grad,
    rel_index,
    attn_weight,
    attn_first,
    attn_second,
    proj_weight,
    proj_first,
    proj_second,
    up_weight,
    up_first,
    up_second,
    down_weight,
    down_first,
    down_second,
    vectors,
    vec_first,
    vec_second,
    head_bias,
    head_first,
    head_second,
    unit_bias,
    unit_first,
    unit_second,
    rel_table,
    table_first,
    table_second,
):
    def flat(field):
        return jnp.transpose(field, (1, 2, 0, 3)).reshape(1568, 512)

    def unflat(rows):
        return jnp.transpose(rows.reshape(14, 14, 8, 512), (2, 0, 1, 3))

    def turned(a):
        return jnp.transpose(a, (1, 0, 2))

    def row(a):
        return a.reshape(1, 512)

    def same(a):
        return a

    def flipped(a):
        return a.T

    ways = (turned, flipped, same, flipped, same, same, row, flipped)
    back = (turned, flipped, same, flipped, same, same, lambda a: a.reshape(512), flipped)
    groups = (
        (attn_weight, attn_first, attn_second),
        (proj_weight, proj_first, proj_second),
        (up_weight, up_first, up_second),
        (down_weight, down_first, down_second),
        (vectors, vec_first, vec_second),
        (head_bias, head_first, head_second),
        (unit_bias, unit_first, unit_second),
        (rel_table, table_first, table_second),
    )
    states = [way(a) for way, group in zip(ways, groups) for a in group]
    attn, proj, up, down, vec, head, unit, rel = states[::3]
    block, igrad, *grads = run_block(
        flat(images), flat(out_grad), vec, rel_index, attn, proj, up, down, rel, head, unit
    )
    block, igrad, *new = update((block, igrad), grads, states)
    news = [way(a) for way, at in zip(back, range(0, 24, 3)) for a in new[at : at + 3]]
    return (unflat(block), unflat(igrad), *news)


def solution(mesh):
    in_specs = (
        P("fsdp", None, None, None),
        P("fsdp", None, None, None),
        P(),
        P("fsdp", None, "tensor"),
        P("fsdp", None, "tensor"),
        P("fsdp", None, "tensor"),
        P("tensor", "fsdp"),
        P("tensor", "fsdp"),
        P("tensor", "fsdp"),
        P("fsdp", "tensor"),
        P("fsdp", "tensor"),
        P("fsdp", "tensor"),
        P("tensor", "fsdp"),
        P("tensor", "fsdp"),
        P("tensor", "fsdp"),
        P(),
        P(),
        P(),
        P(None, "tensor"),
        P(None, "tensor"),
        P(None, "tensor"),
        P("tensor"),
        P("tensor"),
        P("tensor"),
        P(None, "tensor"),
        P(None, "tensor"),
        P(None, "tensor"),
    )
    out_specs = (
        P("fsdp", None, None, None),
        P("fsdp", None, None, None),
        P("fsdp", None, "tensor"),
        P("fsdp", None, "tensor"),
        P("fsdp", None, "tensor"),
        P("tensor", "fsdp"),
        P("tensor", "fsdp"),
        P("tensor", "fsdp"),
        P("fsdp", "tensor"),
        P("fsdp", "tensor"),
        P("fsdp", "tensor"),
        P("tensor", "fsdp"),
        P("tensor", "fsdp"),
        P("tensor", "fsdp"),
        P(),
        P(),
        P(),
        P(None, "tensor"),
        P(None, "tensor"),
        P(None, "tensor"),
        P("tensor"),
        P("tensor"),
        P("tensor"),
        P(None, "tensor"),
        P(None, "tensor"),
        P(None, "tensor"),
    )
    return jax.shard_map(
        on_device, mesh=mesh, in_specs=in_specs, out_specs=out_specs, check_vma=False
    )
```

```python
import types

import jax
import jax.numpy as jnp
from jax import lax
from jax.experimental import pallas as pl
from jax.experimental.pallas import tpu as pltpu
from jax.sharding import PartitionSpec as P

MESH = pl.DeviceIdType.MESH
LOW = jnp.bfloat16
FULL = jnp.float32
EPS = 1e-5
SCALE = 32.0 ** -0.5
BLOCKED = -1e30
STEP = 10
REL = 169
BETA_ONE = 0.9
BETA_TWO = 0.999
ADAM_EPS = 1e-08
RATE_MATRIX = 0.1
RATE_VECTOR = 0.2
RATE_TABLE = 0.5
WEIGHT_DECAY = 0.05
ORDERS = ((0, 1, 2), (1, 2, 0), (2, 0, 1))
SUMS = (((0, 1, 2), (1, 0, 2), (1, 0, 2)), ((0, 1, 2), (1, 0, 2), (0, 1, 2)))
WIDTHS = (128, 384)


class Place:
    def __init__(self):
        f = lax.axis_index("fsdp")
        self.t = lax.axis_index("tensor")
        x, y = f % 4, f // 8
        z = ((f // 4) % 2) * 2 + self.t // 2
        self.core = self.t % 2
        self.at = (x, y, z)
        mate = (x, y, (z // 2) * 2 + 1 - z % 2)
        self.sibling = self.device(core=1 - self.core)
        self.z_mate = self.device(mate)
        self.across = self.device(mate, 1 - self.core)
        self.mate_t = (1 - z % 2) * 2 + self.core

    def device(self, at=None, core=None):
        x, y, z = self.at if at is None else at
        core = self.core if core is None else core
        return (y * 8 + (z // 2) * 4 + x, (z % 2) * 2 + core)

    def along(self, axis, by):
        at = list(self.at)
        at[axis] = (at[axis] + by + 4) % 4
        return self.device(at)


def block_of(ref, lead, place, core, full, axis=None, shift=0, half=None):
    whole = slice(None)
    at = list(place.at)
    if axis is not None:
        at[axis] = (at[axis] + shift + 4) % 4
    x, y, z = at
    x = whole if 0 in full else x
    y = whole if 1 in full else y
    low, high = (whole, whole) if 2 in full else (z % 2, z // 2)
    low = low if half is None else half
    return ref.at[(*lead, low, core, y, high, x)] if core is not None else ref.at[(*lead, low, y, high, x)]


def block_dims(full):
    return tuple(size for axis, size in ((2, 2), (1, 4), (2, 2), (0, 4)) if axis in full)


def each(dims, fn):
    outer = dims[:-1]
    count = 1
    for size in outer:
        count *= size
    if count == 1:
        fn((0,) * len(outer))
        return

    def body(n, _):
        index = []
        for size in reversed(outer):
            index.append(n % size)
            n = n // size
        fn(tuple(reversed(index)))
        return 0

    lax.fori_loop(0, count, body, 0)


def mm(a, b):
    return lax.dot_general(a, b, (((1,), (0,)), ((), ())), preferred_element_type=FULL)


def mm_nt(a, b):
    return lax.dot_general(a, b, (((1,), (1,)), ((), ())), preferred_element_type=FULL)


def mm_tn(a, b):
    return lax.dot_general(a, b, (((0,), (0,)), ((), ())), preferred_element_type=FULL)


def three_lows(a):
    high = a.astype(LOW)
    rest = a - high.astype(FULL)
    middle = rest.astype(LOW)
    last = (rest - middle.astype(FULL)).astype(LOW)
    return jnp.concatenate([high, middle, last], axis=0)


def normed(v):
    center = v - jnp.mean(v, axis=-1, keepdims=True)
    r = lax.rsqrt(jnp.mean(center * center, axis=-1, keepdims=True) + EPS)
    return center * r, r


def norm_back(n, x, r, offset):
    q = n * (1.0 + offset)
    return r * (q - jnp.mean(q, axis=-1, keepdims=True) - x * jnp.mean(q * x, axis=-1, keepdims=True))


def gelu_parts(u):
    size = jnp.abs(u)
    k = 1.0 / (1.0 + (0.3275911 * 0.7071067811865476) * size)
    bell = jnp.exp(-0.5 * u * u)
    poly = k * (0.254829592 + k * (-0.284496736 + k * (1.421413741 + k * (-1.453152027 + k * 1.061405429))))
    tail = 0.5 * poly * bell
    share = jnp.where(u < 0, tail, 1.0 - tail)
    return u * share, share + u * bell * 0.3989422804014327


def lane_mask(h):
    lane = lax.broadcasted_iota(jnp.int32, (128, 128), 1)
    return (lane >= h * 32) & (lane < h * 32 + 32)


def keep(mask, a):
    return jnp.where(mask, a, jnp.zeros_like(a))


def spans():
    for image in range(2):
        for r in range(14):
            for side in range(2):
                window = image * 4 + (r // 7) * 2 + side
                yield image, r * 14 + side * 7, window * 64 + (r % 7) * 7


def block_kernel(ref):
    images, cotangents, vec, idx = ref.images, ref.cotangents, ref.vec, ref.idx
    w = (ref.w1, ref.w2)
    g = (ref.g1, ref.g2)
    sib = (ref.sib1, ref.sib2)
    gs, small, steps = ref.gs, ref.small, ref.steps
    tok, cot, cot_low, cot_t = ref.tok, ref.cot, ref.cot_low, ref.cot_t
    n1, n1_t, x1, r1 = ref.n1, ref.n1_t, ref.x1, ref.r1
    n2, n2_t, x2, r2 = ref.n2, ref.n2_t, ref.x2, ref.r2
    qkv, probs, att, mid, hid, gpre = ref.qkv, ref.probs, ref.att, ref.mid, ref.hid, ref.gpre
    gmid, gml, gml_t, dqkv = ref.gmid, ref.gml, ref.gml_t, ref.dqkv
    onehot, spread, bias, dsum, table = ref.onehot, ref.spread, ref.bias, ref.dsum, ref.table
    stage, field, outs = ref.stage, ref.field, ref.outs
    local = ref.local_sem

    place = Place()
    t_own, core = place.t, place.core
    barrier = pltpu.get_barrier_semaphore()
    partners = [place.along(axis, by) for axis in range(3) for by in (1, 2, 3)] + [place.sibling, place.across]
    for device in partners:
        pl.semaphore_signal(barrier, inc=1, device_id=device, device_id_type=MESH)

    copies_in = [
        pltpu.make_async_copy(images, ref.img, local.at[0]),
        pltpu.make_async_copy(cotangents, ref.cimg, local.at[1]),
    ]
    for copy in copies_in:
        copy.start()

    sends = []

    def send(src, dst, out, into, device):
        copy = pltpu.make_async_remote_copy(src, dst, out, into, device, MESH)
        copy.start()
        sends.append(copy)

    def wait_in(block, out, into):
        pltpu.make_async_remote_copy(block, block, out, into, place.sibling, MESH).wait_recv()

    x, y, z = place.at
    own = (z % 2, core, y, z // 2, x)
    for p in range(3):
        w[0][(p, *own)] = ref.attn[p].astype(LOW)
    proj, up, down = ref.proj[...].astype(LOW), ref.up[...].astype(LOW), ref.down[...].astype(LOW)
    w[1][(0, *own)] = jnp.concatenate([proj, up[:, 0:256]], axis=1)
    w[1][(1, *own)] = jnp.concatenate([up[:, 256:512], down[:, 0:128]], axis=1)
    w[1][(2, *own)] = down[:, 128:512]
    mine = gs.at[t_own]
    mine[...] = jnp.zeros((16, 128), FULL)
    mine[0:4, :] = ref.rel[:, 0:128]
    mine[4:8, 0 : REL - 128] = ref.rel[:, 128:REL]
    mine[8:10, :] = ref.head[...]
    for k in range(4):
        mine[10 + k : 11 + k, :] = ref.unit[:, k * 128 : (k + 1) * 128]

    pl.semaphore_wait(barrier, len(partners))

    in_sem, out_sem, sib_in, sib_out = ref.w_in, ref.w_out, ref.ws_in, ref.ws_out

    def gather_start(b, phase):
        for p in range(3):
            axis, done = ORDERS[p][phase], ORDERS[p][:phase]
            block = block_of(w[b], (p,), place, core, done)
            for shift in (1, 3, 2):
                at = (b, p, phase, shift - 1)
                send(block, block, out_sem.at[at], in_sem.at[at], place.along(axis, shift))
            if phase == 2:
                send(block, block, sib_out.at[b, p, 0], sib_in.at[b, p, 0], place.sibling)

    def gather_finish(b, phase, shifts=(1, 3, 2)):
        for shift in shifts:
            for p in range(3):
                axis, done = ORDERS[p][phase], ORDERS[p][:phase]
                block = block_of(w[b], (p,), place, core, done, axis, -shift)
                at = (b, p, phase, shift - 1)
                wait_in(block, out_sem.at[at], in_sem.at[at])
                if phase == 2:
                    send(block, block, sib_out.at[b, p, shift], sib_in.at[b, p, shift], place.sibling)

    def gather_last(b, groups=(0, 1, 2)):
        for p in groups:
            axis, done = ORDERS[p][2], ORDERS[p][:2]
            for shift in range(4):
                block = block_of(w[b], (p,), place, 1 - core, done, axis, -shift)
                wait_in(block, sib_out.at[b, p, shift], sib_in.at[b, p, shift])

    mates = (place.sibling, place.z_mate, place.across)
    mate_ts = (t_own + 1 - 2 * core, place.mate_t, (1 - z % 2) * 2 + 1 - core)
    gather_start(0, 0)
    gather_start(1, 0)
    for k in range(3):
        send(mine, mine, ref.s_out.at[k], ref.s_in.at[k], mates[k])

    wide = ref.wide
    wide[...] = jnp.full((56, 128), -1, jnp.int32)
    wide[0:49, 0:49] = idx[...]
    wide[0:49, 64:113] = idx[...]
    row_id = lax.broadcasted_iota(jnp.int32, (256, 128), 0)
    for i in range(49):
        onehot[:, i * 128 : (i + 1) * 128] = (row_id == wide[i : i + 1, :]).astype(FULL).astype(LOW)
    small[...] = jnp.zeros((16, 768), FULL)
    tok[...] = jnp.zeros((512, 512), FULL)
    cot[...] = jnp.zeros((512, 512), FULL)
    gather_finish(0, 0)
    gather_start(0, 1)
    gather_finish(1, 0)
    gather_start(1, 1)
    for n, (source, copy, dst) in enumerate(zip((ref.img, ref.cimg), copies_in, (tok, cot))):
        copy.wait()
        if n == 1:
            gather_finish(0, 1)
            gather_start(0, 2)
            gather_finish(1, 1)

        def widen(k, _):
            rows = pl.ds(pl.multiple_of(k * 112, 112), 112)
            for k4 in range(4):
                stage[k4, rows, :] = source[rows, k4 * 128 : (k4 + 1) * 128].astype(FULL)
            return 0

        lax.fori_loop(0, 14, widen, 0)
        for image, first, top in spans():
            for k in range(4):
                dst[top : top + 7, k * 128 : (k + 1) * 128] = stage[
                    k, pl.ds(first * 8 + image + 2 * t_own, 7, stride=8), :
                ]
    gather_finish(0, 2, (1, 3))
    gather_start(1, 2)

    def start(k, _):
        rows = pl.ds(pl.multiple_of(k * 64, 64), 64)
        xs, r = normed(tok[rows, :])
        x1[rows, :] = xs
        r1[rows, :] = r
        n1[rows, :] = (xs * (1.0 + vec[0:1, :]) + vec[1:2, :]).astype(LOW)
        c = cot[rows, :]
        cot_low[rows, :] = c.astype(LOW)
        small[5:6, 0:512] += jnp.sum(c, axis=0, keepdims=True)
        return 0

    lax.fori_loop(0, 8, start, 0)
    n1_t[...] = n1[...].T
    cot_t[...] = cot_low[...].T
    gather_finish(0, 2, (2,))
    for k in range(3):
        wait_in(gs.at[mate_ts[k]], ref.s_out.at[k], ref.s_in.at[k])
    for t in range(4):
        table[t * 4 : t * 4 + 4, 0:128] = gs[t, 0:4, :]
        table[t * 4 : t * 4 + 4, 128:256] = gs[t, 4:8, :]
    spread[...] = mm(three_lows(table[...]), onehot[...])
    lane = lax.broadcasted_iota(jnp.int32, (16, 128), 1)
    low_side = lane < 49
    high_side = (lane >= 64) & (lane < 113)
    for i in range(64):
        if i < 49:
            at = slice(i * 128, (i + 1) * 128)
            line = spread[0:16, at] + spread[16:32, at] + spread[32:48, at]
        else:
            line = jnp.zeros((16, 128), FULL)
        bias[i * 16 : (i + 1) * 16, :] = jnp.where(low_side, line, BLOCKED)
        bias[(64 + i) * 16 : (65 + i) * 16, :] = jnp.where(high_side, line, BLOCKED)
    gather_last(0)

    def columns(b, p, t, a, z):
        return w[b][p, t // 2, t % 2, :, :, :, :, a:z].reshape(512, z - a)

    def w_qkv(t):
        return jnp.concatenate([columns(0, c, t, 0, 128) for c in range(3)], axis=1)

    def w_proj(t):
        return columns(1, 0, t, 0, 128)

    def w_up(t):
        return jnp.concatenate([columns(1, 0, t, 128, 384), columns(1, 1, t, 0, 256)], axis=1)

    def w_down(t):
        return jnp.concatenate([columns(1, 1, t, 256, 384), columns(1, 2, t, 0, 384)], axis=1)

    def put_grad(b, p, t, a, value):
        g[b][p, t // 2, t % 2, :, :, :, :, a : a + value.shape[1]] = value.astype(LOW).reshape(
            4, 2, 4, 16, value.shape[1]
        )

    near = ref.near

    def by_head(a):
        return jnp.concatenate([keep(lane_mask(h), a) for h in range(4)], axis=0)

    def heads_wide(a):
        return jnp.concatenate([a[h * 128 : (h + 1) * 128] for h in range(4)], axis=1)

    def forward(t, _):
        mixed = mm(n1[...], w_qkv(t))
        q_bias, v_bias = gs[t, 8:9, :], gs[t, 9:10, :]
        qkv[t, 0] = (mixed[:, 0:128] + q_bias).astype(LOW)
        qkv[t, 1] = mixed[:, 128:256].astype(LOW)
        qkv[t, 2] = (mixed[:, 256:384] + v_bias).astype(LOW)
        for h in range(4):
            near[h * 128 : (h + 1) * 128, :] = bias[pl.ds(t * 4 + h, 128, stride=16), :]
        for wp in range(4):
            rows = slice(wp * 128, (wp + 1) * 128)
            q, k, v = qkv[t, 0, rows], qkv[t, 1, rows], qkv[t, 2, rows]
            s = mm_nt(by_head(q), k) * SCALE + near[...]
            e = jnp.exp(s - jnp.max(s, axis=-1, keepdims=True))
            p = (e * (1.0 / jnp.sum(e, axis=-1, keepdims=True))).astype(LOW)
            probs[t, wp] = p
            att[t, rows] = mm(heads_wide(p), by_head(v)).astype(LOW)
        return 0

    lax.fori_loop(0, 3, forward, 0)
    gather_finish(1, 2, (1, 3))
    lax.fori_loop(3, 4, forward, 0)
    gather_finish(1, 2, (2,))
    gather_last(1, (0,))

    def second(k, _):
        rows = pl.ds(pl.multiple_of(k * 128, 128), 128)
        acc = tok[rows, :] + (mid[rows, :] + vec[2:3, :])
        mid[rows, :] = acc
        xs, r = normed(acc)
        x2[rows, :] = xs
        r2[rows, :] = r
        n2[rows, :] = (xs * (1.0 + vec[3:4, :]) + vec[4:5, :]).astype(LOW)
        return 0

    mid[...] = mm_nt(
        jnp.concatenate([att[t] for t in range(4)], axis=1), jnp.concatenate([w_proj(t) for t in range(4)], axis=1)
    )
    lax.fori_loop(0, 4, second, 0)
    gmid[...] = jnp.zeros((512, 512), FULL)
    n2_t[...] = n2[...].T
    gather_last(1, (1, 2))

    ghid = ref.ghid

    def feed(t, _):
        unit = jnp.concatenate([gs[t, 10 + k : 11 + k, :] for k in range(4)], axis=1)
        up_t, down_t = w_up(t), w_down(t)

        tok[...] = mm(n2[...], up_t) + unit
        ghid[...] = mm(cot_low[...], down_t)

        def rows_of(k, total):
            rows = pl.ds(pl.multiple_of(k * 64, 64), 64)
            value, slope = gelu_parts(tok[rows, :])
            hid[t, rows, :] = value.astype(LOW)
            grad = ghid[rows, :] * slope
            gpre[t, rows, :] = grad.astype(LOW)
            return total + jnp.sum(grad, axis=0, keepdims=True)

        small[pl.ds(8 + t, 1), 0:512] = lax.fori_loop(0, 8, rows_of, jnp.zeros((1, 512), FULL))
        grad_up = mm(n2_t[...], gpre[t])
        put_grad(1, 0, t, 128, grad_up[:, 0:256])
        put_grad(1, 1, t, 0, grad_up[:, 256:512])
        grad_down = mm(cot_t[...], hid[t])
        put_grad(1, 1, t, 256, grad_down[:, 0:128])
        put_grad(1, 2, t, 0, grad_down[:, 128:512])
        mid[...] += mm_nt(hid[t], down_t)
        gmid[...] += mm_nt(gpre[t], up_t)
        return 0

    g_in, g_out, gs_in, gs_out = ref.g_in, ref.g_out, ref.gs_in, ref.gs_out
    slot = ref.slots

    def sum_core(b, p, half):
        axis, full = SUMS[b][p][0], SUMS[b][p][1:]
        for shift in (1, 3, 2, 0):
            src = block_of(g[b], (p,), place, 1 - core, full, axis, shift, half)
            dst = block_of(sib[b], (p,), place, None, full, axis, shift, half)
            send(src, dst, gs_out.at[b, p, shift, half], gs_in.at[b, p, shift, half], place.sibling)

    def sum_first(b, p, half):
        axis, full = SUMS[b][p][0], SUMS[b][p][1:]
        for shift in (1, 3, 2, 0):
            here = block_of(g[b], (p,), place, core, full, axis, shift, half)
            there = block_of(sib[b], (p,), place, None, full, axis, shift, half)
            wait_in(there, gs_out.at[b, p, shift, half], gs_in.at[b, p, shift, half])

            def add(index):
                here[index] = here[index] + there[index]

            each(block_dims(full)[1:], add)
            if shift:
                at = (b, p, 0, shift - 1, half)
                send(here, slot[b, p, 0].at[shift - 1, half], g_out.at[at], g_in.at[at], place.along(axis, shift))

    def sum_start(b, p, phase):
        axis, full = SUMS[b][p][phase], SUMS[b][p][phase + 1 :]
        for shift in (1, 3, 2):
            here = block_of(g[b], (p,), place, core, full, axis, shift)
            at = (b, p, phase, shift - 1, 0)
            send(here, slot[b, p, phase].at[shift - 1], g_out.at[at], g_in.at[at], place.along(axis, shift))

    def sum_finish(b, p, phase):
        axis, full = SUMS[b][p][phase], SUMS[b][p][phase + 1 :]
        here = block_of(g[b], (p,), place, core, full)
        came = [slot[b, p, phase].at[k] for k in range(3)]
        for k in range(3):
            for half in range(2 if phase == 0 else 1):
                at = (b, p, phase, k, half)
                wait_in(came[k].at[half] if phase == 0 else came[k], g_out.at[at], g_in.at[at])

        def total(index):
            one, two, three = (c[index].astype(FULL) for c in came)
            return (here[index].astype(FULL) + one) + (two + three)

        if phase == 2:
            return total(())

        def add(index):
            here[index] = total(index).astype(LOW)

        each(block_dims(full), add)
        return None

    lax.fori_loop(0, 2, feed, 0)
    for p in (1, 2):
        sum_core(1, p, 0)
    lax.fori_loop(2, 3, feed, 0)
    for p in (1, 2):
        sum_first(1, p, 0)
    lax.fori_loop(3, 4, feed, 0)
    for p in (1, 2):
        sum_core(1, p, 1)

    def third(k, _):
        rows = pl.ds(pl.multiple_of(k * 128, 128), 128)
        mid[rows, :] += vec[5:6, :]
        n = gmid[rows, :]
        xs = x2[rows, :]
        grad = cot[rows, :] + norm_back(n, xs, r2[rows, :], vec[3:4, :])
        gmid[rows, :] = grad
        gml[rows, :] = grad.astype(LOW)
        small[2:3, 0:512] += jnp.sum(grad, axis=0, keepdims=True)
        small[3:4, 0:512] += jnp.sum(n * xs, axis=0, keepdims=True)
        small[4:5, 0:512] += jnp.sum(n, axis=0, keepdims=True)
        return 0

    lax.fori_loop(0, 4, third, 0)
    for p in (1, 2):
        sum_first(1, p, 1)
    gml_t[...] = gml[...].T

    def proj_grad(t, _):
        put_grad(1, 0, t, 0, mm(gml_t[...], att[t]))
        return 0

    lax.fori_loop(0, 4, proj_grad, 0)
    for half in range(2):
        sum_core(1, 0, half)

    o_in, o_out = ref.o_in, ref.o_out

    def give(n, half, src):
        rows = pl.ds(half * 208, 208)
        for image, first, top in spans():
            if image == half:
                field[half * 208 + first : half * 208 + first + 7, :] = src[top : top + 7, :]
        outs[n, t_own, rows, :] = field[rows, :].astype(LOW)
        block = outs.at[n, t_own, rows]
        send(block, block, o_out.at[n, half, 1], o_in.at[n, half, 1], place.z_mate)
        send(block, block, o_out.at[n, half, 0], o_in.at[n, half, 0], place.sibling)

    def came(n, half, kind):
        t = mate_ts[kind]
        block = outs.at[n, t, pl.ds(half * 208, 208)]
        wait_in(block, o_out.at[n, half, kind], o_in.at[n, half, kind])
        if kind == 1:
            send(block, block, o_out.at[n, half, 2], o_in.at[n, half, 2], place.sibling)

    def take(n, half, t):
        field[0:208, :] = outs[n, t, half * 208 : half * 208 + 208, :].astype(FULL)
        for k in range(4):
            stage[k, pl.ds(2 * t + half, 196, stride=8), :] = field[0:196, k * 128 : (k + 1) * 128]

    def take_near(n):
        for half in range(2):
            take(n, half, t_own)
            came(n, half, 0)
            take(n, half, mate_ts[0])

    def take_far(n):
        for half in range(2):
            take(n, half, mate_ts[1])
        for half in range(2):
            came(n, half, 2)
            take(n, half, mate_ts[2])

    field[...] = jnp.zeros((416, 512), FULL)
    give(0, 0, mid)
    give(0, 1, mid)
    for half in range(2):
        sum_first(1, 0, half)

    def backward(image, t):
        span = slice(image * 256, image * 256 + 256)
        ga = mm(gml[span, :], w_proj(t)).astype(LOW)
        sums = jnp.zeros((512, 128), FULL)
        sum_q = jnp.zeros((1, 128), FULL)
        sum_v = jnp.zeros((1, 128), FULL)
        for n in range(2):
            wp = image * 2 + n
            rows = slice(wp * 128, (wp + 1) * 128)
            q, k, v = qkv[t, 0, rows], qkv[t, 1, rows], qkv[t, 2, rows]
            grad = by_head(ga[n * 128 : (n + 1) * 128])
            p_low = probs[t, wp]
            p = p_low.astype(FULL)
            dp = mm_nt(grad, v)
            ds = (p * (dp - jnp.sum(dp * p, axis=-1, keepdims=True))).astype(LOW)
            sums = sums + ds.astype(FULL)
            dq = (mm(heads_wide(ds), by_head(k)) * SCALE).astype(LOW)
            dk = (mm_tn(ds, by_head(q)) * SCALE).astype(LOW)
            dv = mm_tn(p_low, grad).astype(LOW)
            dqkv[t, rows, 0:128] = dq
            dqkv[t, rows, 128:256] = dk
            dqkv[t, rows, 256:384] = dv
            sum_q = sum_q + jnp.sum(dq.astype(FULL), axis=0, keepdims=True)
            sum_v = sum_v + jnp.sum(dv.astype(FULL), axis=0, keepdims=True)
        for h in range(4):
            at = pl.ds(t * 4 + h, 128, stride=16)
            value = sums[h * 128 : (h + 1) * 128]
            dsum[at, :] = value + dsum[at, :] if image else value
        at = pl.ds(pl.multiple_of(t * 128, 128), 128)
        small[6:7, at] += sum_q
        small[7:8, at] += sum_v
        tok[span, :] += mm_nt(dqkv[t, span, :], w_qkv(t))
        if image:
            grad = mm(n1_t[...], dqkv[t])
            for c in range(3):
                put_grad(0, c, t, 0, grad[:, c * 128 : (c + 1) * 128])

    def backward_first(t, _):
        backward(0, t)
        return 0

    def backward_second(t, _):
        backward(1, t)
        return 0

    def last(k, _):
        rows = pl.ds(pl.multiple_of(k * 128, 128), 128)
        n = tok[rows, :]
        xs = x1[rows, :]
        gmid[rows, :] += norm_back(n, xs, r1[rows, :], vec[0:1, :])
        small[0:1, 0:512] += jnp.sum(n * xs, axis=0, keepdims=True)
        small[1:2, 0:512] += jnp.sum(n, axis=0, keepdims=True)
        return 0

    tok[...] = jnp.zeros((512, 512), FULL)
    lax.fori_loop(0, 4, backward_first, 0)
    lax.fori_loop(0, 2, last, 0)
    give(1, 0, gmid)
    lax.fori_loop(0, 2, backward_second, 0)
    for p in range(3):
        sum_core(0, p, 0)
    lax.fori_loop(2, 3, backward_second, 0)
    for p in range(3):
        sum_first(0, p, 0)
    lax.fori_loop(3, 4, backward_second, 0)
    for p in range(3):
        sum_core(0, p, 1)
    lax.fori_loop(2, 4, last, 0)
    give(1, 1, gmid)
    for p in range(3):
        sum_first(0, p, 1)
    lines = []
    for i in range(49):
        lines.append(three_lows(dsum[i * 16 : (i + 1) * 16, :] + dsum[(64 + i) * 16 : (65 + i) * 16, :]))
    table_sum = mm_nt(jnp.concatenate(lines, axis=1), onehot[...])
    small[:, 512:768] = table_sum[0:16] + table_sum[16:32] + table_sum[32:48]

    n_in, n_out = ref.n_in, ref.n_out

    def small_start(k):
        if k < 3:
            block = steps.at[k, place.at[k]]
            for shift in (1, 3, 2):
                send(block, block, n_out.at[k, shift - 1], n_in.at[k, shift - 1], place.along(k, shift))
        else:
            block = steps.at[3, core]
            send(block, block, n_out.at[3, 0], n_in.at[3, 0], place.sibling)

    def small_finish(k):
        if k < 3:
            for shift in (1, 3, 2):
                at = (place.at[k] - shift + 4) % 4
                wait_in(steps.at[k, at], n_out.at[k, shift - 1], n_in.at[k, shift - 1])
            return (steps[k, 0] + steps[k, 1]) + (steps[k, 2] + steps[k, 3])
        wait_in(steps.at[3, 1 - core], n_out.at[3, 0], n_in.at[3, 0])
        return steps[3, 0] + steps[3, 1]

    def small_next(k):
        value = small_finish(k)
        steps[k + 1, place.at[k + 1] if k < 2 else core] = value
        small_start(k + 1)

    steps[0, place.at[0]] = small[...]
    small_start(0)
    for half in range(2):
        came(0, half, 1)
    came(1, 0, 1)
    for p in range(3):
        sum_finish(0, p, 0)
        sum_start(0, p, 1)
    small_next(0)
    take_near(0)
    for p in range(3):
        sum_finish(1, p, 0)
        sum_start(1, p, 1)
    take_far(0)

    def narrow(k, _):
        rows = pl.ds(pl.multiple_of(k * 112, 112), 112)
        for k4 in range(4):
            ref.block_out[rows, k4 * 128 : (k4 + 1) * 128] = stage[k4, rows, :].astype(LOW)
        return 0

    lax.fori_loop(0, 14, narrow, 0)
    for p in range(3):
        sum_finish(0, p, 1)
        sum_start(0, p, 2)
    small_next(1)
    for p in range(3):
        sum_finish(1, p, 1)
        sum_start(1, p, 2)
    take_near(1)
    came(1, 1, 1)
    for p in range(3):
        ref.attn_grad[p] = sum_finish(0, p, 2)
    small_next(2)
    first, second_, third_ = (sum_finish(1, p, 2) for p in range(3))
    ref.proj_grad[...] = first[:, 0:128]
    ref.up_grad[:, 0:256] = first[:, 128:384]
    ref.up_grad[:, 256:512] = second_[:, 0:256]
    ref.down_grad[:, 0:128] = second_[:, 256:384]
    ref.down_grad[:, 128:512] = third_
    take_far(1)
    ref.total[...] = small_finish(3)
    results = []
    for k in range(4):
        lanes = ref.images_grad.at[:, pl.ds(k * 128, 128)]
        results.append(pltpu.make_async_copy(stage.at[k], lanes, local.at[k]))
        results[k].start()
    for copy in sends:
        copy.wait_send()
    for copy in results:
        copy.wait()


def run_block(images, cotangents, vec, idx, attn, proj, up, down, rel, head, unit):
    whole = pl.BlockSpec(memory_space=pltpu.VMEM)
    anywhere = pl.BlockSpec(memory_space=pl.ANY)
    ins = dict(
        images=anywhere, cotangents=anywhere, vec=whole, idx=whole, attn=whole, proj=whole,
        up=whole, down=whole, rel=whole, head=whole, unit=whole,
    )
    results = dict(
        block_out=((1568, 512), LOW, whole),
        images_grad=((1568, 512), FULL, anywhere),
        attn_grad=((3, 16, 128), FULL, whole),
        proj_grad=((16, 128), FULL, whole),
        up_grad=((16, 512), FULL, whole),
        down_grad=((16, 512), FULL, whole),
        total=((16, 768), FULL, whole),
    )
    square = (512, 512)
    scratch = dict(
        img=pltpu.VMEM((1568, 512), LOW),
        cimg=pltpu.VMEM((1568, 512), LOW),
        w1=pltpu.VMEM((3, 2, 2, 4, 2, 4, 16, 128), LOW),
        w2=pltpu.VMEM((3, 2, 2, 4, 2, 4, 16, 384), LOW),
        g1=pltpu.VMEM((3, 2, 2, 4, 2, 4, 16, 128), LOW),
        g2=pltpu.VMEM((3, 2, 2, 4, 2, 4, 16, 384), LOW),
        sib1=pltpu.VMEM((3, 2, 4, 2, 4, 16, 128), LOW),
        sib2=pltpu.VMEM((3, 2, 4, 2, 4, 16, 384), LOW),
        gs=pltpu.VMEM((4, 16, 128), FULL),
        small=pltpu.VMEM((16, 768), FULL),
        steps=pltpu.VMEM((4, 4, 16, 768), FULL),
        qkv=pltpu.VMEM((4, 3, 512, 128), LOW),
        probs=pltpu.VMEM((4, 4, 512, 128), LOW),
        att=pltpu.VMEM((4, 512, 128), LOW),
        hid=pltpu.VMEM((4, 512, 512), LOW),
        gpre=pltpu.VMEM((4, 512, 512), LOW),
        dqkv=pltpu.VMEM((4, 512, 384), LOW),
        onehot=pltpu.VMEM((256, 49 * 128), LOW),
        spread=pltpu.VMEM((48, 49 * 128), FULL),
        bias=pltpu.VMEM((2048, 128), FULL),
        dsum=pltpu.VMEM((2048, 128), FULL),
        table=pltpu.VMEM((16, 256), FULL),
        wide=pltpu.VMEM((56, 128), jnp.int32),
        near=pltpu.VMEM((512, 128), FULL),
        stage=pltpu.VMEM((4, 1568, 128), FULL),
        field=pltpu.VMEM((416, 512), FULL),
        outs=pltpu.VMEM((2, 4, 416, 512), LOW),
        r1=pltpu.VMEM((512, 1), FULL),
        r2=pltpu.VMEM((512, 1), FULL),
    )
    full, low = pltpu.VMEM(square, FULL), pltpu.VMEM(square, LOW)
    scratch.update(ghid=full, tok=full, cot=full, x1=full, x2=full, mid=full, gmid=full)
    scratch.update(cot_low=low, cot_t=low, n1=low, n1_t=low, n2=low, n2_t=low, gml=low, gml_t=low)
    slots = {}
    for b in range(2):
        for p in range(3):
            for phase in range(3):
                slots[b, p, phase] = pltpu.VMEM((3, *block_dims(SUMS[b][p][phase + 1 :]), 16, WIDTHS[b]), LOW)
    sems = dict(
        local_sem=(4,), w_in=(2, 3, 3, 3), w_out=(2, 3, 3, 3), ws_in=(2, 3, 4), ws_out=(2, 3, 4),
        s_in=(3,), s_out=(3,), g_in=(2, 3, 3, 3, 2), g_out=(2, 3, 3, 3, 2), gs_in=(2, 3, 4, 2), gs_out=(2, 3, 4, 2),
        o_in=(2, 2, 3), o_out=(2, 2, 3), n_in=(4, 3), n_out=(4, 3),
    )
    for name, shape in sems.items():
        scratch[name] = pltpu.SemaphoreType.DMA(shape)
    names = [*ins, *results, *scratch]

    def kernel(*refs):
        named = dict(zip(names, refs))
        block_kernel(types.SimpleNamespace(**named, slots=dict(zip(slots, refs[len(names) :]))))

    return pl.pallas_call(
        kernel,
        out_shape=tuple(jax.ShapeDtypeStruct(shape, dtype) for shape, dtype, _ in results.values()),
        in_specs=list(ins.values()),
        out_specs=[spec for _, _, spec in results.values()],
        scratch_shapes=[*scratch.values(), *slots.values()],
        compiler_params=pltpu.CompilerParams(
            collective_id=0, has_side_effects=True, vmem_limit_bytes=63 * 2**20
        ),
        name="block_forward_backward",
    )(images, cotangents, vec, idx, attn, proj, up, down, rel, head, unit)


def adam_step(weight, grad, first, second, rate, decay):
    first_new = BETA_ONE * first + (1.0 - BETA_ONE) * grad
    second_new = BETA_TWO * second + (1.0 - BETA_TWO) * grad * grad
    first_hat = first_new / (1.0 - BETA_ONE**STEP)
    second_hat = second_new / (1.0 - BETA_TWO**STEP)
    updated = weight - rate * (first_hat / (jnp.sqrt(second_hat) + ADAM_EPS) + decay * weight)
    return (updated, first_new, second_new)


PARAMETERS = (
    ((3, 16, 128), RATE_MATRIX, WEIGHT_DECAY),
    ((16, 128), RATE_MATRIX, WEIGHT_DECAY),
    ((16, 512), RATE_MATRIX, WEIGHT_DECAY),
    ((16, 512), RATE_MATRIX, WEIGHT_DECAY),
    ((6, 512), RATE_VECTOR, 0.0),
    ((2, 128), RATE_VECTOR, 0.0),
    ((1, 512), RATE_VECTOR, 0.0),
    ((4, REL), RATE_TABLE, 0.0),
)


def update_kernel(*refs):
    refs = list(refs)

    def some(count):
        taken = refs[:count]
        del refs[:count]
        return taken

    results, grads, states = some(2), some(5), some(24)
    results_out, states_out = some(2), some(24)
    held, grads_in, states_in, states_new = some(2), some(5), some(24), some(24)
    sems_in, sems_out = refs
    arriving = []
    leaving = []
    for n, (source, page, target) in enumerate(zip(results, held, results_out)):
        for k in range(2):
            rows = pl.ds(k * 784, 784)
            at = 2 * n + k
            arriving.append(pltpu.make_async_copy(source.at[rows], page.at[rows], sems_in.at[29 + at]))
            leaving.append(pltpu.make_async_copy(page.at[rows], target.at[rows], sems_out.at[24 + at]))
    loads = [
        pltpu.make_async_copy(a, b, sems_in.at[n]) for n, (a, b) in enumerate(zip(grads + states, grads_in + states_in))
    ]
    for copy in loads + arriving:
        copy.start()
    for copy in loads:
        copy.wait()
    t = lax.axis_index("tensor")
    total = grads_in[4]

    def picked(pieces):
        value = pieces[3]
        for k in (2, 1, 0):
            value = jnp.where(t == k, pieces[k], value)
        return value

    small = (
        total[0:6, 0:512],
        picked([total[6:8, k * 128 : (k + 1) * 128] for k in range(4)]),
        picked([total[8 + k : 9 + k, 0:512] for k in range(4)]),
        picked([total[4 * k : 4 * k + 4, 512 : 512 + REL] for k in range(4)]),
    )
    for coming, going in zip(arriving, leaving):
        coming.wait()
        going.start()
    stores = []
    for n, (_, rate, decay) in enumerate(PARAMETERS):
        grad = grads_in[n][...] if n < 4 else small[n - 4]
        weight, first, second = (states_in[3 * n + k][...] for k in range(3))
        for k, value in enumerate(adam_step(weight, grad, first, second, rate, decay)):
            at = 3 * n + k
            states_new[at][...] = value
            copy = pltpu.make_async_copy(states_new[at], states_out[at], sems_out.at[at])
            copy.start()
            stores.append(copy)
    for copy in stores + leaving:
        copy.wait()


def update(results, grads, states):
    anywhere = pl.BlockSpec(memory_space=pl.ANY)
    shapes = [shape for shape, _, _ in PARAMETERS for _ in range(3)]
    inner = [pltpu.VMEM(shape, FULL) for shape in shapes]
    out_shape = [jax.ShapeDtypeStruct(a.shape, a.dtype) for a in results]
    out_shape += [jax.ShapeDtypeStruct(shape, FULL) for shape in shapes]
    return pl.pallas_call(
        update_kernel,
        out_shape=out_shape,
        in_specs=[anywhere] * 31,
        out_specs=[anywhere] * 26,
        scratch_shapes=[
            *[pltpu.VMEM(a.shape, a.dtype) for a in [*results, *grads]], *inner, *inner,
            pltpu.SemaphoreType.DMA((33,)), pltpu.SemaphoreType.DMA((28,)),
        ],
        compiler_params=pltpu.CompilerParams(vmem_limit_bytes=60 * 2**20),
        name="adam_update",
    )(*results, *grads, *states)


def on_device(
    images,
    out_grad,
    rel_index,
    attn_weight,
    attn_first,
    attn_second,
    proj_weight,
    proj_first,
    proj_second,
    up_weight,
    up_first,
    up_second,
    down_weight,
    down_first,
    down_second,
    vectors,
    vec_first,
    vec_second,
    head_bias,
    head_first,
    head_second,
    unit_bias,
    unit_first,
    unit_second,
    rel_table,
    table_first,
    table_second,
):
    def flat(field):
        return jnp.transpose(field, (1, 2, 0, 3)).reshape(1568, 512)

    def unflat(rows):
        return jnp.transpose(rows.reshape(14, 14, 8, 512), (2, 0, 1, 3))

    def turned(a):
        return jnp.transpose(a, (1, 0, 2))

    def row(a):
        return a.reshape(1, 512)

    def same(a):
        return a

    def flipped(a):
        return a.T

    ways = (turned, flipped, same, flipped, same, same, row, flipped)
    back = (turned, flipped, same, flipped, same, same, lambda a: a.reshape(512), flipped)
    groups = (
        (attn_weight, attn_first, attn_second),
        (proj_weight, proj_first, proj_second),
        (up_weight, up_first, up_second),
        (down_weight, down_first, down_second),
        (vectors, vec_first, vec_second),
        (head_bias, head_first, head_second),
        (unit_bias, unit_first, unit_second),
        (rel_table, table_first, table_second),
    )
    states = [way(a) for way, group in zip(ways, groups) for a in group]
    attn, proj, up, down, vec, head, unit, rel = states[::3]
    block, igrad, *grads = run_block(
        flat(images), flat(out_grad), vec, rel_index, attn, proj, up, down, rel, head, unit
    )
    block, igrad, *new = update((block, igrad), grads, states)
    news = [way(a) for way, at in zip(back, range(0, 24, 3)) for a in new[at : at + 3]]
    return (unflat(block), unflat(igrad), *news)


def solution(mesh):
    in_specs = (
        P("fsdp", None, None, None),
        P("fsdp", None, None, None),
        P(),
        P("fsdp", None, "tensor"),
        P("fsdp", None, "tensor"),
        P("fsdp", None, "tensor"),
        P("tensor", "fsdp"),
        P("tensor", "fsdp"),
        P("tensor", "fsdp"),
        P("fsdp", "tensor"),
        P("fsdp", "tensor"),
        P("fsdp", "tensor"),
        P("tensor", "fsdp"),
        P("tensor", "fsdp"),
        P("tensor", "fsdp"),
        P(),
        P(),
        P(),
        P(None, "tensor"),
        P(None, "tensor"),
        P(None, "tensor"),
        P("tensor"),
        P("tensor"),
        P("tensor"),
        P(None, "tensor"),
        P(None, "tensor"),
        P(None, "tensor"),
    )
    out_specs = (
        P("fsdp", None, None, None),
        P("fsdp", None, None, None),
        P("fsdp", None, "tensor"),
        P("fsdp", None, "tensor"),
        P("fsdp", None, "tensor"),
        P("tensor", "fsdp"),
        P("tensor", "fsdp"),
        P("tensor", "fsdp"),
        P("fsdp", "tensor"),
        P("fsdp", "tensor"),
        P("fsdp", "tensor"),
        P("tensor", "fsdp"),
        P("tensor", "fsdp"),
        P("tensor", "fsdp"),
        P(),
        P(),
        P(),
        P(None, "tensor"),
        P(None, "tensor"),
        P(None, "tensor"),
        P("tensor"),
        P("tensor"),
        P("tensor"),
        P(None, "tensor"),
        P(None, "tensor"),
        P(None, "tensor"),
    )
    return jax.shard_map(
        on_device, mesh=mesh, in_specs=in_specs, out_specs=out_specs, check_vma=False
    )
```
